32 devices in a mesh: dp: 4 (over y, x), ctx: 8 (over z, core).
Axes of the slice: x: 2, y: 2, z: 4, core: 2. Of those that a mesh axis runs over, the one named last changes fastest.
Arguments:
- query_rows: bfloat16 [4, 1024, 2048], P('dp', 'ctx'), may hold values from -6 to 6
- key_rows: bfloat16 [4, 1024, 2048], P('dp', 'ctx'), may hold values from -6 to 6
- value_rows: bfloat16 [4, 1024, 2048], P('dp', 'ctx'), may hold values from -6 to 6
- norm_gain: float32 [2048], replicated, may hold values from 0.1 to 1.9
- out_weight: bfloat16 [2048, 2048], P('ctx'), may hold values from -0.125 to 0.125
- cotangent: bfloat16 [4, 1024, 2048], P('dp', 'ctx'), may hold values from -6 to 6
Outputs:
- mixed: bfloat16 [4, 1024, 2048], P('dp', 'ctx')
- grad_queries: bfloat16 [4, 1024, 2048], P('dp', 'ctx')
- grad_keys: bfloat16 [4, 1024, 2048], P('dp', 'ctx')
- grad_values: bfloat16 [4, 1024, 2048], P('dp', 'ctx')
- grad_weight: float32 [2048, 2048], P('ctx')
The draws below stay inside these ranges and needn't reach their ends.
All inputs are finite; a program needn't handle non-finite values.
Results may differ from the reference program's by a relative error of at most 0.025.
Values may be sent and summed in bfloat16 or wider, within the bound.
No kernel may reach another device: no remote copies, remote signals or barrier semaphores. Data moves between devices by JAX's collectives and lax.ppermute only.
A program may use at most 192 MiB of HBM per device.

```python
import math
import jax
import jax.numpy as jnp
from jax import lax

HEADS = 16
HEAD = 128
D = 2048
SPAN = 128
SEQS = 4
LEN = 1024


def steps_of(key, extent, split, least, top_value):
    def one(axis_at, parts):
        heights = jax.random.uniform(jax.random.fold_in(jax.random.fold_in(key, 6), axis_at), (parts,), jnp.float32, least / len(split), top_value / len(split))
        return jnp.repeat(jnp.exp(heights), extent[axis_at] // parts).reshape((-1,) + (1,) * (len(extent) - axis_at - 1))

    factor_of = one(*split[0])
    for cut in split[1:]:
        factor_of = factor_of * one(*cut)
    return factor_of


def scatter_about(rng, shape, spread, reach, cuts=(), held_as=jnp.bfloat16):
    drawn = spread * jax.random.normal(rng, shape, jnp.float32)
    if cuts:
        drawn = drawn * steps_of(rng, shape, cuts, -0.22, 0.18)
    return jnp.clip(drawn, -reach, reach).astype(held_as)


def setup_inputs(seed: int = 0) -> dict:
    seeds = jax.random.split(jax.random.key(seed), 7)
    return {
        "query_rows": scatter_about(seeds[0], (SEQS, LEN, D), 1.0, 6.0, ((0, 4), (1, 8))),
        "key_rows": scatter_about(seeds[1], (SEQS, LEN, D), 1.0, 6.0, ((0, 4), (1, 8))),
        "value_rows": scatter_about(seeds[2], (SEQS, LEN, D), 1.0, 6.0, ((0, 4), (1, 8))),
        "norm_gain": jnp.clip(1.0 + 0.18 * jax.random.normal(seeds[3], (D,), jnp.float32), 0.1, 1.9),
        "out_weight": scatter_about(seeds[4], (D, D), D ** -0.5, 0.125, ((0, 8),)),
        "cotangent": scatter_about(seeds[5], (SEQS, LEN, D), 1.0, 6.0, ((0, 4), (1, 8))),
    }


epsilon = 1e-06
highest_precision = lax.Precision.HIGHEST

def feature(values):
    wide = values.astype(jnp.float32)
    return jnp.where(wide > 0, wide + 1.0, jnp.exp(jnp.minimum(wide, 0.0))).astype(jnp.bfloat16)

def feature_slope(values):
    wide = values.astype(jnp.float32)
    return jnp.where(wide > 0, 1.0, jnp.exp(jnp.minimum(wide, 0.0)))

def round_trip(values):
    return lax.optimization_barrier(values.astype(jnp.bfloat16)).astype(jnp.float32)

def one_sequence(query_seq, key_seq, value_seq, norm_gain, out_weight, upstream):
    length = query_seq.shape[0]
    blocks = length // SPAN
    shape4 = (blocks, SPAN, HEADS, HEAD)
    query_feat = feature(query_seq).astype(jnp.float32).reshape(shape4)
    key_feat = feature(key_seq).astype(jnp.float32).reshape(shape4)
    value_wide_rows = value_seq.astype(jnp.float32).reshape(shape4)
    local_state = jnp.einsum('cshk,cshv->chkv', key_feat, value_wide_rows, precision=highest_precision)
    running = jnp.cumsum(local_state, axis=0)
    prefix_state = jnp.concatenate([jnp.zeros_like(local_state[:1]), running[:-1]], axis=0)
    causal = jnp.tril(jnp.ones((SPAN, SPAN), dtype=bool))
    scores = jnp.einsum('cthd,cshd->chts', query_feat, key_feat, precision=highest_precision)
    probs = round_trip(jnp.where(causal, scores, 0.0))
    attended_output = jnp.einsum('chts,cshv->cthv', probs, value_wide_rows, precision=highest_precision)
    attended_output = attended_output + jnp.einsum('cthk,chkv->cthv', query_feat, prefix_state, precision=highest_precision)
    inverse = lax.rsqrt(lax.optimization_barrier(jnp.mean(attended_output * attended_output, axis=-1, keepdims=True)) + epsilon)
    gain_heads = norm_gain.astype(jnp.float32).reshape(HEADS, HEAD)
    normed = (attended_output * inverse * gain_heads).reshape(length, D).astype(jnp.bfloat16)
    mixed = jnp.dot(normed, out_weight, preferred_element_type=jnp.float32).astype(jnp.bfloat16)
    d_normed = lax.dot_general(upstream, out_weight, (((1,), (1,)), ((), ())), preferred_element_type=jnp.float32).reshape(shape4)
    scaled = d_normed * gain_heads
    attended_gradient = round_trip(inverse * (scaled - attended_output * inverse * inverse * lax.optimization_barrier(jnp.mean(scaled * attended_output, axis=-1, keepdims=True))))
    grad_local = jnp.einsum('cthk,cthv->chkv', query_feat, attended_gradient, precision=highest_precision)
    backward_run = jnp.cumsum(grad_local[::-1], axis=0)[::-1]
    suffix_state = jnp.concatenate([backward_run[1:], jnp.zeros_like(grad_local[:1])], axis=0)
    d_probs = round_trip(jnp.where(causal, jnp.einsum('cthv,cshv->chts', attended_gradient, value_wide_rows, precision=highest_precision), 0.0))
    query_gradient = jnp.einsum('chts,cshk->cthk', d_probs, key_feat, precision=highest_precision)
    query_gradient = query_gradient + jnp.einsum('cthv,chkv->cthk', attended_gradient, prefix_state, precision=highest_precision)
    key_gradient = jnp.einsum('chts,cthk->cshk', d_probs, query_feat, precision=highest_precision)
    key_gradient = key_gradient + jnp.einsum('cshv,chkv->cshk', value_wide_rows, suffix_state, precision=highest_precision)
    value_gradient = jnp.einsum('chts,cthv->cshv', probs, attended_gradient, precision=highest_precision)
    value_gradient = value_gradient + jnp.einsum('cshk,chkv->cshv', key_feat, suffix_state, precision=highest_precision)
    grad_queries = (query_gradient.reshape(length, D) * feature_slope(query_seq)).astype(jnp.bfloat16)
    grad_keys = (key_gradient.reshape(length, D) * feature_slope(key_seq)).astype(jnp.bfloat16)
    grad_values = value_gradient.reshape(length, D).astype(jnp.bfloat16)
    partial_grad = lax.dot_general(normed, upstream, (((0,), (0,)), ((), ())), preferred_element_type=jnp.float32)
    return (mixed, grad_queries, grad_keys, grad_values, partial_grad)

def reference(query_rows, key_rows, value_rows, norm_gain, out_weight, cotangent):

    def per_sequence(total, pieces):
        query_seq, key_seq, value_seq, upstream = pieces
        mixed, grad_queries, grad_keys, grad_values, partial_grad = one_sequence(query_seq, key_seq, value_seq, norm_gain, out_weight, upstream)
        return (total + partial_grad, (mixed, grad_queries, grad_keys, grad_values))
    total, stacked = lax.scan(per_sequence, jnp.zeros((D, D), jnp.float32), (query_rows, key_rows, value_rows, cotangent))
    grad_weight = total * (1.0 / math.sqrt(SEQS * LEN))
    return (stacked[0], stacked[1], stacked[2], stacked[3], grad_weight)
```

```python
import functools
import math

import jax
import jax.numpy as jnp
from jax import lax
from jax.experimental import pallas as pl
from jax.experimental.pallas import tpu as pltpu
from jax.sharding import PartitionSpec as P

HEAD = 128


epsilon = 1e-06
highest_precision = lax.Precision.HIGHEST


def carried_in(value, axis, combine, identity):
    size, index = (lax.axis_size(axis), lax.axis_index(axis))
    everything = lax.all_gather(value, axis)
    start = jnp.broadcast_to(jnp.asarray(identity, value.dtype), value.shape)

    def carried_turn(k, before):
        reached = k < index
        new = combine(before, everything[k])
        return jnp.where(reached, new, before)

    return lax.fori_loop(0, size, carried_turn, start)


def entering(value, axis, combine, identity):
    size, index = (lax.axis_size(axis), lax.axis_index(axis))
    everything = lax.all_gather(value.astype(jnp.bfloat16), axis)
    start = jnp.broadcast_to(jnp.asarray(identity, value.dtype), value.shape)

    def entering_turn(k, before):
        at = size - 1 - k
        reached = at > index
        new = combine(before, everything[at].astype(value.dtype))
        return jnp.where(reached, new, before)

    return lax.fori_loop(0, size, entering_turn, start)


def feature(values):
    wide = values.astype(jnp.float32)
    return jnp.where(wide > 0, wide + 1.0, jnp.exp(jnp.minimum(wide, 0.0))).astype(jnp.bfloat16)


def feature_slope(values):
    wide = values.astype(jnp.float32)
    return jnp.where(wide > 0, 1.0, jnp.exp(jnp.minimum(wide, 0.0)))


def add_states(earlier, later):
    return earlier + later


def on_device_general(query_rows, key_rows, value_rows, norm_gain, out_weight, cotangent):
    length = query_rows.shape[1]
    width = query_rows.shape[2]
    heads = width // HEAD
    shape3 = (length, heads, HEAD)
    weight = lax.all_gather(out_weight, "ctx", axis=0, tiled=True)
    query_seq = query_rows[0]
    key_seq = key_rows[0]
    query_per_head = feature(query_seq).reshape(shape3)
    key_per_head = feature(key_seq).reshape(shape3)
    value_per_head = value_rows[0].reshape(shape3)
    local_state = jnp.einsum(
        "wmx,wmt->mxt", key_per_head, value_per_head, preferred_element_type=jnp.float32
    )
    zero_state = jnp.zeros_like(local_state)
    prefix_state = carried_in(local_state, "ctx", add_states, zero_state)
    causal = jnp.tril(jnp.ones((length, length), dtype=bool))
    scores = jnp.einsum(
        "thd,shd->hts", query_per_head, key_per_head, preferred_element_type=jnp.float32
    )
    probs = jnp.where(causal, scores, 0.0).astype(jnp.bfloat16)
    query_wide_rows = query_per_head.astype(jnp.float32)
    attended_output = jnp.einsum(
        "hts,shv->thv", probs, value_per_head, preferred_element_type=jnp.float32
    )
    attended_output = attended_output + jnp.einsum(
        "wrf,rfp->wrp", query_wide_rows, prefix_state, precision=highest_precision
    )
    inverse = lax.rsqrt(
        jnp.mean(attended_output * attended_output, axis=-1, keepdims=True) + epsilon
    )
    gain_heads = norm_gain.reshape(heads, HEAD)
    normed = (attended_output * inverse * gain_heads).reshape(length, width).astype(jnp.bfloat16)
    mixed = jnp.dot(normed, weight, preferred_element_type=jnp.float32).astype(jnp.bfloat16)
    upstream = cotangent[0]
    d_normed = lax.dot_general(
        upstream, weight, (((1,), (1,)), ((), ())), preferred_element_type=jnp.float32
    ).reshape(shape3)
    scaled = d_normed * gain_heads
    attended_gradient = (
        inverse
        * (
            scaled
            - attended_output
            * inverse
            * inverse
            * jnp.mean(scaled * attended_output, axis=-1, keepdims=True)
        )
    ).astype(jnp.bfloat16)
    grad_local = jnp.einsum(
        "ibg,ibq->bgq", query_per_head, attended_gradient, preferred_element_type=jnp.float32
    )
    suffix_state = entering(grad_local, "ctx", add_states, zero_state)
    d_scores = jnp.einsum(
        "thv,shv->hts", attended_gradient, value_per_head, preferred_element_type=jnp.float32
    )
    d_probs = jnp.where(causal, d_scores, 0.0).astype(jnp.bfloat16)
    wide_gradient = attended_gradient.astype(jnp.float32)
    value_wide_rows = value_per_head.astype(jnp.float32)
    key_wide_rows = key_per_head.astype(jnp.float32)
    query_gradient = jnp.einsum(
        "hts,shk->thk", d_probs, key_per_head, preferred_element_type=jnp.float32
    )
    query_gradient = query_gradient + jnp.einsum(
        "fxn,xpn->fxp", wide_gradient, prefix_state, precision=highest_precision
    )
    key_gradient = jnp.einsum(
        "hts,thk->shk", d_probs, query_per_head, preferred_element_type=jnp.float32
    )
    key_gradient = key_gradient + jnp.einsum(
        "mcu,cxu->mcx", value_wide_rows, suffix_state, precision=highest_precision
    )
    value_gradient = jnp.einsum(
        "hts,thv->shv", probs, attended_gradient, preferred_element_type=jnp.float32
    )
    value_gradient = value_gradient + jnp.einsum(
        "inz,nzc->inc", key_wide_rows, suffix_state, precision=highest_precision
    )
    grad_queries = (query_gradient.reshape(length, width) * feature_slope(query_seq)).astype(
        jnp.bfloat16
    )
    grad_keys = (key_gradient.reshape(length, width) * feature_slope(key_seq)).astype(jnp.bfloat16)
    grad_values = value_gradient.reshape(length, width).astype(jnp.bfloat16)
    devices_dp = lax.axis_size("dp")
    devices_ctx = lax.axis_size("ctx")
    loss_scale = 1.0 / math.sqrt(devices_dp * devices_ctx * length)
    shares = lax.psum_scatter(
        lax.dot_general(
            normed, upstream, (((0,), (0,)), ((), ())), preferred_element_type=jnp.float32
        ).astype(jnp.bfloat16),
        "ctx",
        scatter_dimension=0,
        tiled=True,
    )
    summed = lax.psum(shares, "dp").astype(jnp.float32)
    grad_weight = summed * loss_scale
    return (mixed[None], grad_queries[None], grad_keys[None], grad_values[None], grad_weight)


CHIPS = 4
COLUMNS = 4
PAIR = 2 * HEAD
QUARTER = PAIR // COLUMNS
VMEM_LIMIT = 40 * 1024 * 1024
bf16 = jnp.bfloat16
f32 = jnp.float32


def dims(a, b, ca, cb):
    return lax.dot_general(a, b, (((ca,), (cb,)), ((), ())), preferred_element_type=f32)


def call(kernel, outs, name, args, flops, grid=(), in_specs=None, out_specs=None, scratch=(), aliases=None):
    vmem = pl.BlockSpec(memory_space=pltpu.VMEM)
    smem = pl.BlockSpec(memory_space=pltpu.SMEM)
    if in_specs is None:
        in_specs = [smem if a.dtype == jnp.int32 else vmem for a in args]
    if out_specs is None:
        out_specs = [vmem for _ in outs]
    moved = sum(math.prod(a.shape) * a.dtype.itemsize for a in list(args) + list(outs))
    return pl.pallas_call(
        kernel,
        out_shape=list(outs),
        grid=grid,
        in_specs=in_specs,
        out_specs=out_specs,
        scratch_shapes=list(scratch),
        input_output_aliases=aliases or {},
        compiler_params=pltpu.CompilerParams(vmem_limit_bytes=VMEM_LIMIT),
        cost_estimate=pl.CostEstimate(flops=flops, bytes_accessed=moved, transcendentals=0),
        name=name,
    )(*args)


def like(shape, dtype):
    return jax.ShapeDtypeStruct(shape, dtype)


def chip_of(place, s):
    return lax.rem(place[0] + (CHIPS - s), CHIPS)


def head_lanes(place, chip, j):
    return pl.ds(pl.multiple_of((2 * chip + place[1]) * PAIR + j * HEAD, HEAD), HEAD)


def rows_of(own, sib, lanes):
    return jnp.concatenate([own[:, lanes], sib[:, lanes]], axis=0)


def causal_mask(place, rows, transposed=False):
    core = place[1]

    def position(axis):
        at = lax.broadcasted_iota(jnp.int32, (rows, rows), axis)
        half = rows // 2
        return jnp.where(at < half, at + core * half, at - core * half)

    query, key = (1, 0) if transposed else (0, 1)
    return position(key) <= position(query)


def states_kernel(place, k_own, k_sib, v_own, v_sib, state):
    for chip in range(CHIPS):
        for j in range(2):
            lanes = head_lanes(place, chip, j)
            fk = feature(rows_of(k_own, k_sib, lanes))
            state[2 * chip + j] = dims(fk, rows_of(v_own, v_sib, lanes), 0, 0).astype(bf16)


def attend_kernel(place, q_own, q_sib, k_own, k_sib, v_own, v_sib, near, far, gain, attended, n0, n1, n2, n3):
    rows = 2 * q_own.shape[0]
    mask = causal_mask(place, rows)
    column = place[2]
    low = lax.broadcasted_iota(jnp.int32, (rows, HEAD), 1) < HEAD // 2
    turned = lax.rem(column, 2) == 1
    swapped = column >= 2
    packs = (n0, n1, n2, n3)
    for t in range(CHIPS // 2):
        pieces = []
        for s in (2 * t, 2 * t + 1):
            chip = chip_of(place, s)
            normed = []
            for j in range(2):
                lanes = head_lanes(place, chip, j)
                fq = feature(rows_of(q_own, q_sib, lanes))
                fk = feature(rows_of(k_own, k_sib, lanes))
                value = rows_of(v_own, v_sib, lanes)
                probs = jnp.where(mask, dims(fq, fk, 1, 1), 0.0).astype(bf16)
                prefix = (near[2 * chip + j].astype(f32) + far[2 * chip + j].astype(f32)).astype(bf16)
                out = dims(probs, value, 1, 0) + dims(fq, prefix, 1, 0)
                attended[:, pl.ds(s * PAIR + j * HEAD, HEAD)] = out
                inverse = lax.rsqrt(jnp.mean(out * out, axis=-1, keepdims=True) + epsilon)
                normed.append(out * inverse * gain[:, lanes])
            first = jnp.where(swapped, normed[1], normed[0])
            second = jnp.where(swapped, normed[0], normed[1])
            pieces.append([jnp.where(turned, pltpu.roll(x, HEAD // 2, 1), x) for x in (first, second)])
        for i in range(2):
            a, b = pieces[0][i], pieces[1][i]
            at = pl.ds(t * HEAD, HEAD)
            packs[2 * i][:, at] = jnp.where(low, a, pltpu.roll(b, HEAD // 2, 1)).astype(bf16)
            packs[2 * i + 1][:, at] = jnp.where(low, pltpu.roll(a, HEAD // 2, 1), b).astype(bf16)


def d_normed_kernel(w, *refs):
    cots, outs = refs[: 2 * COLUMNS], refs[2 * COLUMNS :]
    half = cots[0].shape[0]
    weight = w[...]
    for m in range(COLUMNS):
        outs[m][:half] = dims(cots[2 * m][...], weight, 1, 1).astype(bf16)
        outs[m][half:] = dims(cots[2 * m + 1][...], weight, 1, 1).astype(bf16)


def d_attend_kernel(place, q_own, q_sib, attended, gain, r0, r1, r2, r3, d_attended, state):
    rows = 2 * q_own.shape[0]
    column = place[2]
    low = lax.broadcasted_iota(jnp.int32, (rows, HEAD), 1) < HEAD // 2
    turned = lax.rem(column, 2) == 1
    swapped = column >= 2
    packs = (r0, r1, r2, r3)
    for t in range(CHIPS // 2):
        at = pl.ds(t * HEAD, HEAD)
        pieces = [[], []]
        for i in range(2):
            a, b = packs[2 * i][:, at].astype(f32), packs[2 * i + 1][:, at].astype(f32)
            both = (
                jnp.where(low, a, pltpu.roll(b, HEAD // 2, 1)),
                jnp.where(low, pltpu.roll(a, HEAD // 2, 1), b),
            )
            for which in range(2):
                x = both[which]
                pieces[which].append(jnp.where(turned, pltpu.roll(x, HEAD // 2, 1), x))
        for which in range(2):
            s = 2 * t + which
            chip = chip_of(place, s)
            first, second = pieces[which]
            by_head = (jnp.where(swapped, second, first), jnp.where(swapped, first, second))
            for j in range(2):
                lanes = head_lanes(place, chip, j)
                fq = feature(rows_of(q_own, q_sib, lanes))
                here = pl.ds(s * PAIR + j * HEAD, HEAD)
                out = attended[:, here]
                inverse = lax.rsqrt(jnp.mean(out * out, axis=-1, keepdims=True) + epsilon)
                scaled = by_head[j] * gain[:, lanes]
                share = jnp.mean(scaled * out, axis=-1, keepdims=True)
                grad = (inverse * (scaled - out * (inverse * inverse * share))).astype(bf16)
                d_attended[:, here] = grad
                state[2 * chip + j] = dims(fq, grad, 0, 0).astype(bf16)


def inner_kernel(
    place, q_own, q_sib, k_own, k_sib, v_own, v_sib, near, far, d_attended, gq, gq_sib, part_k, part_v
):
    half = q_own.shape[0]
    mask = causal_mask(place, 2 * half)
    mask_t = causal_mask(place, 2 * half, True)
    for s in range(CHIPS):
        chip = chip_of(place, s)
        for j in range(2):
            lanes = head_lanes(place, chip, j)
            here = pl.ds(s * PAIR + j * HEAD, HEAD)
            query = rows_of(q_own, q_sib, lanes)
            fq = feature(query)
            fk = feature(rows_of(k_own, k_sib, lanes))
            value = rows_of(v_own, v_sib, lanes)
            grad = d_attended[:, here]
            prefix = (near[2 * chip + j].astype(f32) + far[2 * chip + j].astype(f32)).astype(bf16)
            d_probs = jnp.where(mask, dims(grad, value, 1, 1), 0.0).astype(bf16)
            d_probs_t = jnp.where(mask_t, dims(value, grad, 1, 1), 0.0).astype(bf16)
            probs_t = jnp.where(mask_t, dims(fk, fq, 1, 1), 0.0).astype(bf16)
            d_fq = dims(d_probs, fk, 1, 0) + dims(grad, prefix, 1, 1)
            out = (d_fq * feature_slope(query)).astype(bf16)
            gq[:, lanes] = out[:half]
            gq_sib[:, pl.ds(pl.multiple_of(chip * PAIR + j * HEAD, HEAD), HEAD)] = out[half:]
            part_k[:, here] = dims(d_probs_t, fq, 1, 0)
            part_v[:, here] = dims(probs_t, grad, 1, 0)


def outer_kernel(place, k_own, k_sib, v_own, v_sib, near, far, part_k, part_v, gk, gv, sent):
    half = k_own.shape[0]
    for s in range(CHIPS):
        chip = chip_of(place, s)
        for j in range(2):
            lanes = head_lanes(place, chip, j)
            here = pl.ds(s * PAIR + j * HEAD, HEAD)
            there = pl.ds(pl.multiple_of(chip * PAIR + j * HEAD, HEAD), HEAD)
            key = rows_of(k_own, k_sib, lanes)
            value = rows_of(v_own, v_sib, lanes)
            suffix = (near[2 * chip + j].astype(f32) + far[2 * chip + j].astype(f32)).astype(bf16)
            d_fk = part_k[:, here] + dims(value, suffix, 1, 1)
            out_k = (d_fk * feature_slope(key)).astype(bf16)
            out_v = (part_v[:, here] + dims(feature(key), suffix, 1, 0)).astype(bf16)
            gk[:, lanes] = out_k[:half]
            gv[:, lanes] = out_v[:half]
            sent[0, :, there] = out_k[half:]
            sent[1, :, there] = out_v[half:]


def fill_kernel(place, *refs):
    n = (len(refs) + 1) // 3
    got, held, outs = refs[:n], refs[n : 2 * n], refs[2 * n :]
    for chip in range(CHIPS):
        pair = pl.ds(chip * PAIR, PAIR)
        own = pl.ds(pl.multiple_of((2 * chip + place[1]) * PAIR, PAIR), PAIR)
        other = pl.ds(pl.multiple_of((2 * chip + 1 - place[1]) * PAIR, PAIR), PAIR)
        for a, b, o in zip(got, held, outs):
            o[:, own] = b[:, own]
            o[:, other] = a[:, pair]


def mixed_kernel(n0, n1, n2, n3, nx, w_own, w_sib, m0, m1, m2, m3):
    half = nx.shape[1]
    for m, (n, out) in enumerate(zip((n0, n1, n2, n3), (m0, m1, m2, m3))):
        out[...] = (dims(n[:half, :], w_own[...], 1, 0) + dims(nx[m], w_sib[...], 1, 0)).astype(out.dtype)


def weight_kernel(*refs):
    packs, cots, outs = refs[:COLUMNS], refs[COLUMNS : 3 * COLUMNS], refs[3 * COLUMNS :]
    half = cots[0].shape[0]
    total = None
    for m in range(COLUMNS):
        for part in range(2):
            term = dims(packs[m][pl.ds(part * half, half), :], cots[2 * m + part][...], 0, 0)
            total = term if total is None else total + term
    for s in range(CHIPS):
        outs[s][...] = total[s * QUARTER : (s + 1) * QUARTER].astype(outs[s].dtype)


def gathered_kernel(scale, place, t0, t1, t2, t3, out):
    for m, t in enumerate((t0, t1, t2, t3)):
        column = lax.bitwise_xor(place[2], m)
        out[pl.ds(pl.multiple_of(column * QUARTER, QUARTER), QUARTER), :] = t[...].astype(f32) * scale


def on_device_planned(query_rows, key_rows, value_rows, norm_gain, out_weight, cotangent):
    query, key, value, cot = query_rows[0], key_rows[0], value_rows[0], cotangent[0]
    half, width = query.shape
    here, column = lax.axis_index("ctx"), lax.axis_index("dp")
    place = jnp.stack([here // 2, here % 2, column]).astype(jnp.int32)
    gain = norm_gain.reshape(1, width)

    def to_sib(x):
        return lax.ppermute(x, "ctx", [(i, i ^ 1) for i in range(2 * CHIPS)])

    def around(x, s):
        pairs = [(2 * c + e, 2 * ((c + s) % CHIPS) + e) for c in range(CHIPS) for e in range(2)]
        return lax.ppermute(x, "ctx", pairs)

    def along(x, s):
        pairs = [(2 * c + e, 2 * (c + s) + e) for c in range(CHIPS) for e in range(2) if 0 <= c + s < CHIPS]
        return lax.ppermute(x, "ctx", pairs)

    def across(x, m):
        return x if m == 0 else lax.ppermute(x, "dp", [(d, d ^ m) for d in range(COLUMNS)])

    key_sib, value_sib, query_sib = to_sib(key), to_sib(value), to_sib(query)
    heads = 2 * CHIPS
    state_shape = like((heads, HEAD, HEAD), bf16)
    state_flops = 2 * heads * 2 * half * HEAD * HEAD

    state = call(states_kernel, [state_shape], "states", (place, key, key_sib, value, value_sib), state_flops)[0]
    near = along(state, 1)
    far = along(state + near, 2)

    quarter = lax.dynamic_slice(out_weight, (column * QUARTER, 0), (QUARTER, width))
    weight = jnp.concatenate([quarter] + [around(quarter, s) for s in range(1, CHIPS)], axis=0)
    weight_sib = to_sib(weight)
    cots = [across(cot, m) for m in range(COLUMNS)]
    cot_parts = [x for c in cots for x in (c, to_sib(c))]

    pack = like((2 * half, PAIR), bf16)
    attended, *packs = call(
        attend_kernel,
        [like((2 * half, heads * HEAD), f32)] + [pack] * COLUMNS,
        "attend",
        (place, query, query_sib, key, key_sib, value, value_sib, near, far, gain),
        8 * state_flops,
    )
    d_packs = call(
        d_normed_kernel, [pack] * COLUMNS, "d_normed", (weight, *cot_parts), 2 * 8 * half * PAIR * width
    )
    d_got = [across(d_packs[m], m) for m in range(COLUMNS)]
    n_got = [across(packs[m], m) for m in range(COLUMNS)]

    d_attended, d_state = call(
        d_attend_kernel,
        [like((2 * half, heads * HEAD), bf16), state_shape],
        "d_attend",
        (place, query, query_sib, attended, gain, *d_got),
        2 * state_flops,
    )
    d_near = along(d_state, -1)
    d_far = along(d_state + d_near, -2)

    term = like((QUARTER, width), bf16)
    column_spec = lambda rows, step: pl.BlockSpec((rows, step), lambda i: (0, i))
    fixed = lambda shape: pl.BlockSpec(shape, lambda i: (0,) * len(shape))
    step = 512
    terms = call(
        weight_kernel,
        [like((QUARTER, width), f32)] + [term] * (CHIPS - 1),
        "weight_terms",
        (*n_got, *cot_parts),
        2 * 8 * half * PAIR * width,
        grid=(width // step,),
        in_specs=[fixed((2 * half, PAIR))] * COLUMNS + [column_spec(half, step)] * (2 * COLUMNS),
        out_specs=[column_spec(QUARTER, step)] * CHIPS,
    )
    arrived = [around(terms[s], -s) for s in range(1, CHIPS)]
    share = terms[0]
    for x in arrived:
        share = share + x.astype(f32)
    share = share.astype(bf16)
    devices = lax.axis_size("dp") * lax.axis_size("ctx")
    scale = 1.0 / math.sqrt(devices * half)

    n_sib = to_sib(jnp.stack([n[half:] for n in n_got]))
    outs = call(
        mixed_kernel,
        [like((half, width), f32)] + [like((half, width), bf16)] * (COLUMNS - 1),
        "mixed_terms",
        (*n_got, n_sib, weight, weight_sib),
        2 * 4 * half * 2 * PAIR * width,
        grid=(width // step,),
        in_specs=[fixed((2 * half, PAIR))] * COLUMNS
        + [fixed((COLUMNS, half, PAIR))]
        + [column_spec(PAIR, step)] * 2,
        out_specs=[column_spec(half, step)] * COLUMNS,
    )
    mixed = outs[0]
    for m in range(1, COLUMNS):
        mixed = mixed + across(outs[m], m).astype(f32)
    mixed = mixed.astype(bf16)

    full = like((half, width), bf16)
    gq, gq_sent, part_k, part_v = call(
        inner_kernel,
        [full, like((half, width // 2), bf16)] + [like((2 * half, heads * HEAD), f32)] * 2,
        "inner",
        (place, query, query_sib, key, key_sib, value, value_sib, near, far, d_attended),
        14 * state_flops,
    )
    gk, gv, kv_sent = call(
        outer_kernel,
        [full, full, like((2, half, width // 2), bf16)],
        "outer",
        (place, key, key_sib, value, value_sib, d_near, d_far, part_k, part_v),
        2 * state_flops,
    )
    gq_got, kv_got = to_sib(gq_sent), to_sib(kv_sent)
    grad_queries, = call(fill_kernel, [full], "fill_q", (place, gq_got, gq), 0)
    grad_keys, grad_values = call(fill_kernel, [full] * 2, "fill_kv", (place, kv_got[0], kv_got[1], gk, gv), 0)

    shares = [across(share, m) for m in range(COLUMNS)]
    grad_weight, = call(
        functools.partial(gathered_kernel, scale),
        [like(out_weight.shape, f32)],
        "grad_weight",
        (place, *shares),
        0,
    )
    return (mixed[None], grad_queries[None], grad_keys[None], grad_values[None], grad_weight)


def on_device(query_rows, key_rows, value_rows, norm_gain, out_weight, cotangent):
    fits = (
        lax.axis_size("dp") == COLUMNS
        and lax.axis_size("ctx") == 2 * CHIPS
        and out_weight.shape[0] == PAIR
        and out_weight.shape[1] == 2 * CHIPS * PAIR
        and query_rows.shape[1] == HEAD
    )
    path = on_device_planned if fits else on_device_general
    return path(query_rows, key_rows, value_rows, norm_gain, out_weight, cotangent)


def solution(mesh):
    return jax.shard_map(
        on_device,
        mesh=mesh,
        in_specs=(
            P("dp", "ctx", None),
            P("dp", "ctx", None),
            P("dp", "ctx", None),
            P(),
            P("ctx", None),
            P("dp", "ctx", None),
        ),
        out_specs=(
            P("dp", "ctx", None),
            P("dp", "ctx", None),
            P("dp", "ctx", None),
            P("dp", "ctx", None),
            P("ctx", None),
        ),
        check_vma=False,
    )
```

```python
import functools
import math

import jax
import jax.numpy as jnp
from jax import lax
from jax.experimental import pallas as pl
from jax.experimental.pallas import tpu as pltpu
from jax.sharding import PartitionSpec as P

HEAD = 128


epsilon = 1e-06
highest_precision = lax.Precision.HIGHEST


def carried_in(value, axis, combine, identity):
    size, index = (lax.axis_size(axis), lax.axis_index(axis))
    everything = lax.all_gather(value, axis)
    start = jnp.broadcast_to(jnp.asarray(identity, value.dtype), value.shape)

    def carried_turn(k, before):
        reached = k < index
        new = combine(before, everything[k])
        return jnp.where(reached, new, before)

    return lax.fori_loop(0, size, carried_turn, start)


def entering(value, axis, combine, identity):
    size, index = (lax.axis_size(axis), lax.axis_index(axis))
    everything = lax.all_gather(value.astype(jnp.bfloat16), axis)
    start = jnp.broadcast_to(jnp.asarray(identity, value.dtype), value.shape)

    def entering_turn(k, before):
        at = size - 1 - k
        reached = at > index
        new = combine(before, everything[at].astype(value.dtype))
        return jnp.where(reached, new, before)

    return lax.fori_loop(0, size, entering_turn, start)


def feature(values):
    wide = values.astype(jnp.float32)
    return jnp.where(wide > 0, wide + 1.0, jnp.exp(jnp.minimum(wide, 0.0))).astype(jnp.bfloat16)


def feature_slope(values):
    wide = values.astype(jnp.float32)
    return jnp.where(wide > 0, 1.0, jnp.exp(jnp.minimum(wide, 0.0)))


def add_states(earlier, later):
    return earlier + later


def on_device_general(query_rows, key_rows, value_rows, norm_gain, out_weight, cotangent):
    length = query_rows.shape[1]
    width = query_rows.shape[2]
    heads = width // HEAD
    shape3 = (length, heads, HEAD)
    weight = lax.all_gather(out_weight, "ctx", axis=0, tiled=True)
    query_seq = query_rows[0]
    key_seq = key_rows[0]
    query_per_head = feature(query_seq).reshape(shape3)
    key_per_head = feature(key_seq).reshape(shape3)
    value_per_head = value_rows[0].reshape(shape3)
    local_state = jnp.einsum(
        "wmx,wmt->mxt", key_per_head, value_per_head, preferred_element_type=jnp.float32
    )
    zero_state = jnp.zeros_like(local_state)
    prefix_state = carried_in(local_state, "ctx", add_states, zero_state)
    causal = jnp.tril(jnp.ones((length, length), dtype=bool))
    scores = jnp.einsum(
        "thd,shd->hts", query_per_head, key_per_head, preferred_element_type=jnp.float32
    )
    probs = jnp.where(causal, scores, 0.0).astype(jnp.bfloat16)
    query_wide_rows = query_per_head.astype(jnp.float32)
    attended_output = jnp.einsum(
        "hts,shv->thv", probs, value_per_head, preferred_element_type=jnp.float32
    )
    attended_output = attended_output + jnp.einsum(
        "wrf,rfp->wrp", query_wide_rows, prefix_state, precision=highest_precision
    )
    inverse = lax.rsqrt(
        jnp.mean(attended_output * attended_output, axis=-1, keepdims=True) + epsilon
    )
    gain_heads = norm_gain.reshape(heads, HEAD)
    normed = (attended_output * inverse * gain_heads).reshape(length, width).astype(jnp.bfloat16)
    mixed = jnp.dot(normed, weight, preferred_element_type=jnp.float32).astype(jnp.bfloat16)
    upstream = cotangent[0]
    d_normed = lax.dot_general(
        upstream, weight, (((1,), (1,)), ((), ())), preferred_element_type=jnp.float32
    ).reshape(shape3)
    scaled = d_normed * gain_heads
    attended_gradient = (
        inverse
        * (
            scaled
            - attended_output
            * inverse
            * inverse
            * jnp.mean(scaled * attended_output, axis=-1, keepdims=True)
        )
    ).astype(jnp.bfloat16)
    grad_local = jnp.einsum(
        "ibg,ibq->bgq", query_per_head, attended_gradient, preferred_element_type=jnp.float32
    )
    suffix_state = entering(grad_local, "ctx", add_states, zero_state)
    d_scores = jnp.einsum(
        "thv,shv->hts", attended_gradient, value_per_head, preferred_element_type=jnp.float32
    )
    d_probs = jnp.where(causal, d_scores, 0.0).astype(jnp.bfloat16)
    wide_gradient = attended_gradient.astype(jnp.float32)
    value_wide_rows = value_per_head.astype(jnp.float32)
    key_wide_rows = key_per_head.astype(jnp.float32)
    query_gradient = jnp.einsum(
        "hts,shk->thk", d_probs, key_per_head, preferred_element_type=jnp.float32
    )
    query_gradient = query_gradient + jnp.einsum(
        "fxn,xpn->fxp", wide_gradient, prefix_state, precision=highest_precision
    )
    key_gradient = jnp.einsum(
        "hts,thk->shk", d_probs, query_per_head, preferred_element_type=jnp.float32
    )
    key_gradient = key_gradient + jnp.einsum(
        "mcu,cxu->mcx", value_wide_rows, suffix_state, precision=highest_precision
    )
    value_gradient = jnp.einsum(
        "hts,thv->shv", probs, attended_gradient, preferred_element_type=jnp.float32
    )
    value_gradient = value_gradient + jnp.einsum(
        "inz,nzc->inc", key_wide_rows, suffix_state, precision=highest_precision
    )
    grad_queries = (query_gradient.reshape(length, width) * feature_slope(query_seq)).astype(
        jnp.bfloat16
    )
    grad_keys = (key_gradient.reshape(length, width) * feature_slope(key_seq)).astype(jnp.bfloat16)
    grad_values = value_gradient.reshape(length, width).astype(jnp.bfloat16)
    devices_dp = lax.axis_size("dp")
    devices_ctx = lax.axis_size("ctx")
    loss_scale = 1.0 / math.sqrt(devices_dp * devices_ctx * length)
    shares = lax.psum_scatter(
        lax.dot_general(
            normed, upstream, (((0,), (0,)), ((), ())), preferred_element_type=jnp.float32
        ).astype(jnp.bfloat16),
        "ctx",
        scatter_dimension=0,
        tiled=True,
    )
    summed = lax.psum(shares, "dp").astype(jnp.float32)
    grad_weight = summed * loss_scale
    return (mixed[None], grad_queries[None], grad_keys[None], grad_values[None], grad_weight)


CHIPS = 4
ORDER = (0, 2, 1, 3)
COLUMNS = 4
PAIR = 2 * HEAD
QUARTER = PAIR // COLUMNS
VMEM_LIMIT = 40 * 1024 * 1024
bf16 = jnp.bfloat16
f32 = jnp.float32


def dims(a, b, ca, cb):
    return lax.dot_general(a, b, (((ca,), (cb,)), ((), ())), preferred_element_type=f32)


def call(kernel, outs, name, args, flops, grid=(), in_specs=None, out_specs=None, scratch=(), hint=1):
    vmem = pl.BlockSpec(memory_space=pltpu.VMEM)
    smem = pl.BlockSpec(memory_space=pltpu.SMEM)
    if in_specs is None:
        in_specs = [smem if a.dtype == jnp.int32 else vmem for a in args]
    if out_specs is None:
        out_specs = [vmem for _ in outs]
    moved = sum(math.prod(a.shape) * a.dtype.itemsize for a in list(args) + list(outs))
    return pl.pallas_call(
        kernel,
        out_shape=list(outs),
        grid=grid,
        in_specs=in_specs,
        out_specs=out_specs,
        scratch_shapes=list(scratch),
        compiler_params=pltpu.CompilerParams(vmem_limit_bytes=VMEM_LIMIT),
        cost_estimate=pl.CostEstimate(flops=flops * hint, bytes_accessed=moved * hint, transcendentals=0),
        name=name,
    )(*args)


def like(shape, dtype):
    return jax.ShapeDtypeStruct(shape, dtype)


def chip_of(place, s):
    return lax.bitwise_xor(place[0], ORDER[s])


def head_lanes(place, chip, j):
    return pl.ds(pl.multiple_of((2 * chip + place[1]) * PAIR + j * HEAD, HEAD), HEAD)


def entering_state(near, far, at, takes_near):
    first = jnp.where(takes_near, near[at].astype(f32), 0.0)
    return (first + far[at].astype(f32)).astype(bf16)


def rows_of(own, sib, lanes):
    return jnp.concatenate([own[:, lanes], sib[:, lanes]], axis=0)


def causal_mask(place, rows, transposed=False):
    core = place[1]

    def position(axis):
        at = lax.broadcasted_iota(jnp.int32, (rows, rows), axis)
        half = rows // 2
        return jnp.where(at < half, at + core * half, at - core * half)

    query, key = (1, 0) if transposed else (0, 1)
    return position(key) <= position(query)


def states_kernel(place, k_own, k_sib, v_own, v_sib, state):
    for chip in range(CHIPS):
        for j in range(2):
            lanes = head_lanes(place, chip, j)
            fk = feature(rows_of(k_own, k_sib, lanes))
            state[2 * chip + j] = dims(fk, rows_of(v_own, v_sib, lanes), 0, 0).astype(bf16)


def attend_kernel(place, q_own, q_sib, k_own, k_sib, v_own, v_sib, near, far, gain, attended, n0, n1, n2, n3):
    rows = 2 * q_own.shape[0]
    mask = causal_mask(place, rows)
    odd = lax.rem(place[0], 2) == 1
    column = place[2]
    low = lax.broadcasted_iota(jnp.int32, (rows, HEAD), 1) < HEAD // 2
    turned = lax.rem(column, 2) == 1
    swapped = column >= 2
    packs = (n0, n1, n2, n3)
    for t in range(CHIPS // 2):
        pieces = []
        for s in (2 * t, 2 * t + 1):
            chip = chip_of(place, s)
            normed = []
            for j in range(2):
                lanes = head_lanes(place, chip, j)
                fq = feature(rows_of(q_own, q_sib, lanes))
                fk = feature(rows_of(k_own, k_sib, lanes))
                value = rows_of(v_own, v_sib, lanes)
                probs = jnp.where(mask, dims(fq, fk, 1, 1), 0.0).astype(bf16)
                prefix = entering_state(near, far, 2 * chip + j, odd)
                out = dims(probs, value, 1, 0) + dims(fq, prefix, 1, 0)
                attended[:, pl.ds(s * PAIR + j * HEAD, HEAD)] = out
                inverse = lax.rsqrt(jnp.mean(out * out, axis=-1, keepdims=True) + epsilon)
                normed.append(out * inverse * gain[:, lanes])
            first = jnp.where(swapped, normed[1], normed[0])
            second = jnp.where(swapped, normed[0], normed[1])
            pieces.append([jnp.where(turned, pltpu.roll(x, HEAD // 2, 1), x) for x in (first, second)])
        for i in range(2):
            a, b = pieces[0][i], pieces[1][i]
            at = pl.ds(t * HEAD, HEAD)
            packs[2 * i][:, at] = jnp.where(low, a, pltpu.roll(b, HEAD // 2, 1)).astype(bf16)
            packs[2 * i + 1][:, at] = jnp.where(low, pltpu.roll(a, HEAD // 2, 1), b).astype(bf16)


def d_normed_kernel(w_first, w_second, *refs):
    cots, outs = refs[: 2 * COLUMNS], refs[2 * COLUMNS :]
    half = cots[0].shape[0]
    weight = jnp.concatenate([w_first[...], w_second[...]], axis=0)
    for m in range(COLUMNS):
        outs[m][:half] = dims(cots[2 * m][...], weight, 1, 1).astype(bf16)
        outs[m][half:] = dims(cots[2 * m + 1][...], weight, 1, 1).astype(bf16)


def d_attend_kernel(place, q_own, q_sib, attended, gain, r0, r1, r2, r3, d_attended, state):
    rows = 2 * q_own.shape[0]
    column = place[2]
    low = lax.broadcasted_iota(jnp.int32, (rows, HEAD), 1) < HEAD // 2
    turned = lax.rem(column, 2) == 1
    swapped = column >= 2
    packs = (r0, r1, r2, r3)
    for t in range(CHIPS // 2):
        at = pl.ds(t * HEAD, HEAD)
        pieces = [[], []]
        for i in range(2):
            a, b = packs[2 * i][:, at].astype(f32), packs[2 * i + 1][:, at].astype(f32)
            both = (
                jnp.where(low, a, pltpu.roll(b, HEAD // 2, 1)),
                jnp.where(low, pltpu.roll(a, HEAD // 2, 1), b),
            )
            for which in range(2):
                x = both[which]
                pieces[which].append(jnp.where(turned, pltpu.roll(x, HEAD // 2, 1), x))
        for which in range(2):
            s = 2 * t + which
            chip = chip_of(place, s)
            first, second = pieces[which]
            by_head = (jnp.where(swapped, second, first), jnp.where(swapped, first, second))
            for j in range(2):
                lanes = head_lanes(place, chip, j)
                fq = feature(rows_of(q_own, q_sib, lanes))
                here = pl.ds(s * PAIR + j * HEAD, HEAD)
                out = attended[:, here]
                inverse = lax.rsqrt(jnp.mean(out * out, axis=-1, keepdims=True) + epsilon)
                scaled = by_head[j] * gain[:, lanes]
                share = jnp.mean(scaled * out, axis=-1, keepdims=True)
                grad = (inverse * (scaled - out * (inverse * inverse * share))).astype(bf16)
                d_attended[:, here] = grad
                state[2 * chip + j] = dims(fq, grad, 0, 0).astype(bf16)


def inner_kernel(
    place, q_own, q_sib, k_own, k_sib, v_own, v_sib, near, far, d_attended, gq, part_k, part_v, sent
):
    half = q_own.shape[0]
    mask = causal_mask(place, 2 * half)
    mask_t = causal_mask(place, 2 * half, True)
    odd = lax.rem(place[0], 2) == 1
    for s in range(CHIPS):
        chip = chip_of(place, s)
        for j in range(2):
            lanes = head_lanes(place, chip, j)
            here = pl.ds(s * PAIR + j * HEAD, HEAD)
            there = pl.ds(pl.multiple_of(chip * PAIR + j * HEAD, HEAD), HEAD)
            query = rows_of(q_own, q_sib, lanes)
            fq = feature(query)
            fk = feature(rows_of(k_own, k_sib, lanes))
            value = rows_of(v_own, v_sib, lanes)
            grad = d_attended[:, here]
            prefix = entering_state(near, far, 2 * chip + j, odd)
            d_probs = jnp.where(mask, dims(grad, value, 1, 1), 0.0).astype(bf16)
            d_probs_t = jnp.where(mask_t, dims(value, grad, 1, 1), 0.0).astype(bf16)
            probs_t = jnp.where(mask_t, dims(fk, fq, 1, 1), 0.0).astype(bf16)
            d_fq = dims(d_probs, fk, 1, 0) + dims(grad, prefix, 1, 1)
            out = (d_fq * feature_slope(query)).astype(bf16)
            from_k = dims(d_probs_t, fq, 1, 0)
            from_v = dims(probs_t, grad, 1, 0)
            gq[:, lanes] = out[:half]
            part_k[:, there] = from_k[:half]
            part_v[:, there] = from_v[:half]
            sent[0, :, there] = out[half:]
            sent[1, :, there] = from_k[half:].astype(bf16)
            sent[2, :, there] = from_v[half:].astype(bf16)


def outer_kernel(place, k_own, v_own, near, near_sib, far, far_sib, part_k, part_v, got, gk, gv):
    odd = lax.rem(place[0], 2) == 1
    for chip in range(CHIPS):
        for j in range(2):
            there = pl.ds(chip * PAIR + j * HEAD, HEAD)
            for other in range(2):
                block = 2 * chip + (1 - place[1] if other else place[1])
                lanes = pl.ds(pl.multiple_of(block * PAIR + j * HEAD, HEAD), HEAD)
                states = (near_sib, far_sib) if other else (near, far)
                suffix = entering_state(*states, 2 * chip + j, jnp.logical_not(odd))
                from_k = got[1, :, there].astype(f32) if other else part_k[:, there]
                from_v = got[2, :, there].astype(f32) if other else part_v[:, there]
                key = k_own[:, lanes]
                d_fk = from_k + dims(v_own[:, lanes], suffix, 1, 1)
                gk[:, lanes] = (d_fk * feature_slope(key)).astype(bf16)
                gv[:, lanes] = (from_v + dims(feature(key), suffix, 1, 0)).astype(bf16)


def fill_kernel(place, got, held, out):
    for chip in range(CHIPS):
        pair = pl.ds(chip * PAIR, PAIR)
        own = pl.ds(pl.multiple_of((2 * chip + place[1]) * PAIR, PAIR), PAIR)
        other = pl.ds(pl.multiple_of((2 * chip + 1 - place[1]) * PAIR, PAIR), PAIR)
        out[:, own] = held[:, own]
        out[:, other] = got[0, :, pair]


def mixed_kernel(n0, n1, n2, n3, nx, w_own, w_sib, m0, m1, m2, m3):
    half = nx.shape[1]
    weight = jnp.concatenate([w_own[...], w_sib[...]], axis=0)
    for m, (n, out) in enumerate(zip((n0, n1, n2, n3), (m0, m1, m2, m3))):
        rows = jnp.concatenate([n[:half, :], nx[m]], axis=1)
        out[...] = dims(rows, weight, 1, 0).astype(out.dtype)


def weight_kernel(*refs):
    packs, cots, outs = refs[:COLUMNS], refs[COLUMNS : 3 * COLUMNS], refs[3 * COLUMNS :]
    half = cots[0].shape[0]
    total = None
    for m in range(COLUMNS):
        for part in range(2):
            term = dims(packs[m][pl.ds(part * half, half), :], cots[2 * m + part][...], 0, 0)
            total = term if total is None else total + term
    outs[0][...] = total[: 2 * QUARTER]
    outs[1][...] = total[2 * QUARTER :].astype(bf16)


def gathered_kernel(scale, place, t0, t1, t2, t3, out):
    for m, t in enumerate((t0, t1, t2, t3)):
        column = lax.bitwise_xor(place[2], m)
        out[pl.ds(pl.multiple_of(column * QUARTER, QUARTER), QUARTER), :] = t[...].astype(f32) * scale


def after(x, *earlier):
    return lax.optimization_barrier((x, *earlier))[0]


def on_device_planned(query_rows, key_rows, value_rows, norm_gain, out_weight, cotangent):
    query, key, value, cot = query_rows[0], key_rows[0], value_rows[0], cotangent[0]
    half, width = query.shape
    here, column = lax.axis_index("ctx"), lax.axis_index("dp")
    place = jnp.stack([here // 2, here % 2, column]).astype(jnp.int32)
    gain = norm_gain.reshape(1, width)
    heads = 2 * CHIPS
    state_shape = like((heads, HEAD, HEAD), bf16)
    state_flops = 2 * heads * 2 * half * HEAD * HEAD
    pack, full = like((2 * half, PAIR), bf16), like((half, width), bf16)
    part = like((half, width // 2), f32)
    step = 512

    def column_spec(rows, columns):
        return pl.BlockSpec((rows, columns), lambda i: (0, i))

    def fixed(shape):
        return pl.BlockSpec(shape, lambda i: (0,) * len(shape))

    def sent(x, name, axis, pairs):
        with jax.named_scope("send_" + name):
            return lax.ppermute(x, axis, pairs)

    def to_sib(x, name):
        return sent(x, name, "ctx", [(i, i ^ 1) for i in range(2 * CHIPS)])

    def swapped(x, s, name):
        pairs = [(2 * c + e, 2 * (c ^ s) + e) for c in range(CHIPS) for e in range(2)]
        return sent(x, name, "ctx", pairs)

    def halfway(x, s, name):
        pairs = [(2 * c + e, 2 * (c + s) + e) for c in range(CHIPS) for e in range(2) if 0 <= c + s < CHIPS]
        return sent(x, name, "ctx", pairs)

    def across(x, m, name):
        return sent(x, name, "dp", [(d, d ^ m) for d in range(COLUMNS)])

    key_sib = to_sib(key, "key")
    value_sib = to_sib(value, "value")
    state = call(
        states_kernel, [state_shape], "states", (place, key, key_sib, value, value_sib), state_flops
    )[0]
    query_sib = to_sib(after(query, state), "query")
    near = swapped(state, 1, "near")
    pair_state = state + near
    far = halfway(pair_state, 2, "far")
    attended, *packs = call(
        attend_kernel,
        [like((2 * half, heads * HEAD), f32)] + [pack] * COLUMNS,
        "attend",
        (place, query, query_sib, key, key_sib, value, value_sib, near, far, gain),
        8 * state_flops,
        hint=0,
    )
    quarter = lax.dynamic_slice(out_weight, (column * QUARTER, 0), (QUARTER, width))
    w2 = swapped(quarter, 2, "w2")
    w_first = jnp.concatenate([quarter, w2], axis=0)
    w_second = swapped(w_first, 1, "w_second")
    sib0 = to_sib(after(cot, state), "sib0")
    cot1 = across(cot, 1, "cot1")
    sib1 = to_sib(cot1, "sib1")
    cot2 = across(cot, 2, "cot2")
    sib2 = to_sib(after(cot2, far), "sib2")
    cot3 = across(after(cot, near), 3, "cot3")
    sib3 = to_sib(cot3, "sib3")
    cot_parts = [cot, sib0, cot1, sib1, cot2, sib2, cot3, sib3]
    d_packs = call(
        d_normed_kernel,
        [pack] * COLUMNS,
        "d_normed",
        (w_first, w_second, *cot_parts),
        2 * 8 * half * PAIR * width,
    )
    n1 = after(across(packs[1], 1, "n1"), *d_packs)
    n2 = after(across(packs[2], 2, "n2"), *d_packs)
    n3 = after(across(packs[3], 3, "n3"), *d_packs)
    n_got = (packs[0], n1, n2, n3)
    kept, given = call(
        weight_kernel,
        [like((2 * QUARTER, width), f32), like((2 * QUARTER, width), bf16)],
        "weight_terms",
        (*n_got, *cot_parts),
        2 * 8 * half * PAIR * width,
        grid=(width // step,),
        in_specs=[fixed((2 * half, PAIR))] * COLUMNS + [column_spec(half, step)] * (2 * COLUMNS),
        out_specs=[column_spec(2 * QUARTER, step)] * 2,
    )
    n_sib = to_sib(after(jnp.stack([n[half:] for n in n_got]), given), "n_sib")
    weight = jnp.concatenate([w_first, w_second], axis=0)
    w_sib = to_sib(after(weight, given), "w_sib")
    outs = call(
        mixed_kernel,
        [like((half, width), f32)] + [like((half, width), bf16)] * (COLUMNS - 1),
        "mixed_terms",
        (*n_got, n_sib, weight, w_sib),
        2 * 4 * half * 2 * PAIR * width,
        grid=(width // step,),
        in_specs=[fixed((2 * half, PAIR))] * COLUMNS
        + [fixed((COLUMNS, half, PAIR))]
        + [column_spec(PAIR, step)] * 2,
        out_specs=[column_spec(half, step)] * COLUMNS,
    )
    mixed1 = across(outs[1], 1, "mixed1")
    mixed2 = across(outs[2], 2, "mixed2")
    mixed3 = across(outs[3], 3, "mixed3")
    mixed_got = [mixed1, mixed2, mixed3]
    mixed = outs[0]
    for x in mixed_got:
        mixed = mixed + x.astype(f32)
    mixed = mixed.astype(bf16)
    d1 = across(after(d_packs[1], given), 1, "d1")
    d2 = across(after(d_packs[2], given), 2, "d2")
    d3 = across(after(d_packs[3], given), 3, "d3")
    d_got = (d_packs[0], d1, d2, d3)
    d_attended, d_state = call(
        d_attend_kernel,
        [like((2 * half, heads * HEAD), bf16), state_shape],
        "d_attend",
        (place, query, query_sib, attended, gain, *d_got),
        2 * state_flops,
    )
    gq, part_k, part_v, parts_sent = call(
        inner_kernel,
        [full, part, part, like((3, half, width // 2), bf16)],
        "inner",
        (place, query, query_sib, key, key_sib, value, value_sib, near, far, after(d_attended, mixed)),
        14 * state_flops,
    )
    parts_got = to_sib(parts_sent, "parts")
    grad_queries = call(fill_kernel, [full], "fill_q", (place, parts_got, gq), 0)[0]
    terms = swapped(given, 1, "terms")
    d_near = swapped(after(d_state, terms), 1, "d_near")
    d_near_sib = to_sib(d_near, "d_near_sib")
    d_pair_state = d_state + d_near
    d_far = halfway(d_pair_state, -2, "d_far")
    d_far_sib = to_sib(d_far, "d_far_sib")
    grad_kv = call(
        outer_kernel,
        [full, full],
        "outer",
        (place, key, value, d_near, d_near_sib, d_far, d_far_sib, part_k, part_v, parts_got),
        2 * state_flops,
    )
    pair = kept + terms.astype(f32)
    pair_terms = after(swapped(pair[QUARTER:].astype(bf16), 2, "pair_terms"), gq)
    share = (pair[:QUARTER] + pair_terms.astype(f32)).astype(bf16)
    share1 = across(share, 1, "share1")
    share2 = across(share, 2, "share2")
    share3 = across(share, 3, "share3")
    scale = 1.0 / math.sqrt(lax.axis_size("dp") * lax.axis_size("ctx") * half)
    grad_weight = call(
        functools.partial(gathered_kernel, scale),
        [like(out_weight.shape, f32)],
        "grad_weight",
        (place, *(share, share1, share2, share3)),
        0,
    )[0]
    return (mixed[None], grad_queries[None], grad_kv[0][None], grad_kv[1][None], grad_weight)


def on_device(query_rows, key_rows, value_rows, norm_gain, out_weight, cotangent):
    fits = (
        lax.axis_size("dp") == COLUMNS
        and lax.axis_size("ctx") == 2 * CHIPS
        and out_weight.shape[0] == PAIR
        and out_weight.shape[1] == 2 * CHIPS * PAIR
        and query_rows.shape[1] == HEAD
    )
    path = on_device_planned if fits else on_device_general
    return path(query_rows, key_rows, value_rows, norm_gain, out_weight, cotangent)


def solution(mesh):
    return jax.shard_map(
        on_device,
        mesh=mesh,
        in_specs=(
            P("dp", "ctx", None),
            P("dp", "ctx", None),
            P("dp", "ctx", None),
            P(),
            P("ctx", None),
            P("dp", "ctx", None),
        ),
        out_specs=(
            P("dp", "ctx", None),
            P("dp", "ctx", None),
            P("dp", "ctx", None),
            P("dp", "ctx", None),
            P("ctx", None),
        ),
        check_vma=False,
    )
```

```python
import functools
import math

import jax
import jax.numpy as jnp
from jax import lax
from jax.experimental import pallas as pl
from jax.experimental.pallas import tpu as pltpu
from jax.sharding import PartitionSpec as P

HEAD = 128


epsilon = 1e-06
highest_precision = lax.Precision.HIGHEST


def carried_in(value, axis, combine, identity):
    size, index = (lax.axis_size(axis), lax.axis_index(axis))
    everything = lax.all_gather(value, axis)
    start = jnp.broadcast_to(jnp.asarray(identity, value.dtype), value.shape)

    def carried_turn(k, before):
        reached = k < index
        new = combine(before, everything[k])
        return jnp.where(reached, new, before)

    return lax.fori_loop(0, size, carried_turn, start)


def entering(value, axis, combine, identity):
    size, index = (lax.axis_size(axis), lax.axis_index(axis))
    everything = lax.all_gather(value.astype(jnp.bfloat16), axis)
    start = jnp.broadcast_to(jnp.asarray(identity, value.dtype), value.shape)

    def entering_turn(k, before):
        at = size - 1 - k
        reached = at > index
        new = combine(before, everything[at].astype(value.dtype))
        return jnp.where(reached, new, before)

    return lax.fori_loop(0, size, entering_turn, start)


def feature(values):
    wide = values.astype(jnp.float32)
    return jnp.where(wide > 0, wide + 1.0, jnp.exp(jnp.minimum(wide, 0.0))).astype(jnp.bfloat16)


def feature_slope(values):
    wide = values.astype(jnp.float32)
    return jnp.where(wide > 0, 1.0, jnp.exp(jnp.minimum(wide, 0.0)))


def add_states(earlier, later):
    return earlier + later


def on_device_general(query_rows, key_rows, value_rows, norm_gain, out_weight, cotangent):
    length = query_rows.shape[1]
    width = query_rows.shape[2]
    heads = width // HEAD
    shape3 = (length, heads, HEAD)
    weight = lax.all_gather(out_weight, "ctx", axis=0, tiled=True)
    query_seq = query_rows[0]
    key_seq = key_rows[0]
    query_per_head = feature(query_seq).reshape(shape3)
    key_per_head = feature(key_seq).reshape(shape3)
    value_per_head = value_rows[0].reshape(shape3)
    local_state = jnp.einsum(
        "wmx,wmt->mxt", key_per_head, value_per_head, preferred_element_type=jnp.float32
    )
    zero_state = jnp.zeros_like(local_state)
    prefix_state = carried_in(local_state, "ctx", add_states, zero_state)
    causal = jnp.tril(jnp.ones((length, length), dtype=bool))
    scores = jnp.einsum(
        "thd,shd->hts", query_per_head, key_per_head, preferred_element_type=jnp.float32
    )
    probs = jnp.where(causal, scores, 0.0).astype(jnp.bfloat16)
    query_wide_rows = query_per_head.astype(jnp.float32)
    attended_output = jnp.einsum(
        "hts,shv->thv", probs, value_per_head, preferred_element_type=jnp.float32
    )
    attended_output = attended_output + jnp.einsum(
        "wrf,rfp->wrp", query_wide_rows, prefix_state, precision=highest_precision
    )
    inverse = lax.rsqrt(
        jnp.mean(attended_output * attended_output, axis=-1, keepdims=True) + epsilon
    )
    gain_heads = norm_gain.reshape(heads, HEAD)
    normed = (attended_output * inverse * gain_heads).reshape(length, width).astype(jnp.bfloat16)
    mixed = jnp.dot(normed, weight, preferred_element_type=jnp.float32).astype(jnp.bfloat16)
    upstream = cotangent[0]
    d_normed = lax.dot_general(
        upstream, weight, (((1,), (1,)), ((), ())), preferred_element_type=jnp.float32
    ).reshape(shape3)
    scaled = d_normed * gain_heads
    attended_gradient = (
        inverse
        * (
            scaled
            - attended_output
            * inverse
            * inverse
            * jnp.mean(scaled * attended_output, axis=-1, keepdims=True)
        )
    ).astype(jnp.bfloat16)
    grad_local = jnp.einsum(
        "ibg,ibq->bgq", query_per_head, attended_gradient, preferred_element_type=jnp.float32
    )
    suffix_state = entering(grad_local, "ctx", add_states, zero_state)
    d_scores = jnp.einsum(
        "thv,shv->hts", attended_gradient, value_per_head, preferred_element_type=jnp.float32
    )
    d_probs = jnp.where(causal, d_scores, 0.0).astype(jnp.bfloat16)
    wide_gradient = attended_gradient.astype(jnp.float32)
    value_wide_rows = value_per_head.astype(jnp.float32)
    key_wide_rows = key_per_head.astype(jnp.float32)
    query_gradient = jnp.einsum(
        "hts,shk->thk", d_probs, key_per_head, preferred_element_type=jnp.float32
    )
    query_gradient = query_gradient + jnp.einsum(
        "fxn,xpn->fxp", wide_gradient, prefix_state, precision=highest_precision
    )
    key_gradient = jnp.einsum(
        "hts,thk->shk", d_probs, query_per_head, preferred_element_type=jnp.float32
    )
    key_gradient = key_gradient + jnp.einsum(
        "mcu,cxu->mcx", value_wide_rows, suffix_state, precision=highest_precision
    )
    value_gradient = jnp.einsum(
        "hts,thv->shv", probs, attended_gradient, preferred_element_type=jnp.float32
    )
    value_gradient = value_gradient + jnp.einsum(
        "inz,nzc->inc", key_wide_rows, suffix_state, precision=highest_precision
    )
    grad_queries = (query_gradient.reshape(length, width) * feature_slope(query_seq)).astype(
        jnp.bfloat16
    )
    grad_keys = (key_gradient.reshape(length, width) * feature_slope(key_seq)).astype(jnp.bfloat16)
    grad_values = value_gradient.reshape(length, width).astype(jnp.bfloat16)
    devices_dp = lax.axis_size("dp")
    devices_ctx = lax.axis_size("ctx")
    loss_scale = 1.0 / math.sqrt(devices_dp * devices_ctx * length)
    shares = lax.psum_scatter(
        lax.dot_general(
            normed, upstream, (((0,), (0,)), ((), ())), preferred_element_type=jnp.float32
        ).astype(jnp.bfloat16),
        "ctx",
        scatter_dimension=0,
        tiled=True,
    )
    summed = lax.psum(shares, "dp").astype(jnp.float32)
    grad_weight = summed * loss_scale
    return (mixed[None], grad_queries[None], grad_keys[None], grad_values[None], grad_weight)


CHIPS = 4
ORDER = (0, 2, 1, 3)
COLUMNS = 4
PAIR = 2 * HEAD
QUARTER = PAIR // COLUMNS
VMEM_LIMIT = 40 * 1024 * 1024
bf16 = jnp.bfloat16
f32 = jnp.float32


def dims(a, b, ca, cb):
    return lax.dot_general(a, b, (((ca,), (cb,)), ((), ())), preferred_element_type=f32)


def call(kernel, outs, name, args, flops, grid=(), in_specs=None, out_specs=None, scratch=(), hint=1):
    vmem = pl.BlockSpec(memory_space=pltpu.VMEM)
    smem = pl.BlockSpec(memory_space=pltpu.SMEM)
    if in_specs is None:
        in_specs = [smem if a.dtype == jnp.int32 else vmem for a in args]
    if out_specs is None:
        out_specs = [vmem for _ in outs]
    moved = sum(math.prod(a.shape) * a.dtype.itemsize for a in list(args) + list(outs))
    return pl.pallas_call(
        kernel,
        out_shape=list(outs),
        grid=grid,
        in_specs=in_specs,
        out_specs=out_specs,
        scratch_shapes=list(scratch),
        compiler_params=pltpu.CompilerParams(vmem_limit_bytes=VMEM_LIMIT),
        cost_estimate=pl.CostEstimate(flops=flops * hint, bytes_accessed=moved * hint, transcendentals=0),
        name=name,
    )(*args)


def like(shape, dtype):
    return jax.ShapeDtypeStruct(shape, dtype)


def chip_of(place, s):
    return lax.bitwise_xor(place[0], ORDER[s])


def head_lanes(place, chip, j):
    return pl.ds(pl.multiple_of((2 * chip + place[1]) * PAIR + j * HEAD, HEAD), HEAD)


def entering_state(near, far, at, takes_near):
    first = jnp.where(takes_near, near[at].astype(f32), 0.0)
    return (first + far[at].astype(f32)).astype(bf16)


def rows_of(own, sib, lanes):
    return jnp.concatenate([own[:, lanes], sib[:, lanes]], axis=0)


def causal_mask(place, rows, transposed=False):
    core = place[1]

    def position(axis):
        at = lax.broadcasted_iota(jnp.int32, (rows, rows), axis)
        half = rows // 2
        return jnp.where(at < half, at + core * half, at - core * half)

    query, key = (1, 0) if transposed else (0, 1)
    return position(key) <= position(query)


def states_kernel(place, k_own, k_sib, v_own, v_sib, state):
    for chip in range(CHIPS):
        for j in range(2):
            lanes = head_lanes(place, chip, j)
            fk = feature(rows_of(k_own, k_sib, lanes))
            state[2 * chip + j] = dims(fk, rows_of(v_own, v_sib, lanes), 0, 0).astype(bf16)


def attend_kernel(place, q_own, q_sib, k_own, k_sib, v_own, v_sib, near, far, gain, attended, n0, n1, n2, n3):
    rows = 2 * q_own.shape[0]
    mask = causal_mask(place, rows)
    odd = lax.rem(place[0], 2) == 1
    column = place[2]
    low = lax.broadcasted_iota(jnp.int32, (rows, HEAD), 1) < HEAD // 2
    turned = lax.rem(column, 2) == 1
    swapped = column >= 2
    packs = (n0, n1, n2, n3)
    for t in range(CHIPS // 2):
        pieces = []
        for s in (2 * t, 2 * t + 1):
            chip = chip_of(place, s)
            normed = []
            for j in range(2):
                lanes = head_lanes(place, chip, j)
                fq = feature(rows_of(q_own, q_sib, lanes))
                fk = feature(rows_of(k_own, k_sib, lanes))
                value = rows_of(v_own, v_sib, lanes)
                probs = jnp.where(mask, dims(fq, fk, 1, 1), 0.0).astype(bf16)
                prefix = entering_state(near, far, 2 * chip + j, odd)
                out = dims(probs, value, 1, 0) + dims(fq, prefix, 1, 0)
                attended[:, pl.ds(s * PAIR + j * HEAD, HEAD)] = out
                inverse = lax.rsqrt(jnp.mean(out * out, axis=-1, keepdims=True) + epsilon)
                normed.append(out * inverse * gain[:, lanes])
            first = jnp.where(swapped, normed[1], normed[0])
            second = jnp.where(swapped, normed[0], normed[1])
            pieces.append([jnp.where(turned, pltpu.roll(x, HEAD // 2, 1), x) for x in (first, second)])
        for i in range(2):
            a, b = pieces[0][i], pieces[1][i]
            at = pl.ds(t * HEAD, HEAD)
            packs[2 * i][:, at] = jnp.where(low, a, pltpu.roll(b, HEAD // 2, 1)).astype(bf16)
            packs[2 * i + 1][:, at] = jnp.where(low, pltpu.roll(a, HEAD // 2, 1), b).astype(bf16)


def d_normed_kernel(w_first, w_second, *refs):
    cots, outs = refs[: 2 * COLUMNS], refs[2 * COLUMNS :]
    half = cots[0].shape[0]
    weight = jnp.concatenate([w_first[...], w_second[...]], axis=0)
    for m in range(COLUMNS):
        outs[m][:half] = dims(cots[2 * m][...], weight, 1, 1).astype(bf16)
        outs[m][half:] = dims(cots[2 * m + 1][...], weight, 1, 1).astype(bf16)


def d_attend_kernel(place, q_own, q_sib, attended, gain, r0, r1, r2, r3, d_attended, state):
    rows = 2 * q_own.shape[0]
    column = place[2]
    low = lax.broadcasted_iota(jnp.int32, (rows, HEAD), 1) < HEAD // 2
    turned = lax.rem(column, 2) == 1
    swapped = column >= 2
    packs = (r0, r1, r2, r3)
    for t in range(CHIPS // 2):
        at = pl.ds(t * HEAD, HEAD)
        pieces = [[], []]
        for i in range(2):
            a, b = packs[2 * i][:, at].astype(f32), packs[2 * i + 1][:, at].astype(f32)
            both = (
                jnp.where(low, a, pltpu.roll(b, HEAD // 2, 1)),
                jnp.where(low, pltpu.roll(a, HEAD // 2, 1), b),
            )
            for which in range(2):
                x = both[which]
                pieces[which].append(jnp.where(turned, pltpu.roll(x, HEAD // 2, 1), x))
        for which in range(2):
            s = 2 * t + which
            chip = chip_of(place, s)
            first, second = pieces[which]
            by_head = (jnp.where(swapped, second, first), jnp.where(swapped, first, second))
            for j in range(2):
                lanes = head_lanes(place, chip, j)
                fq = feature(rows_of(q_own, q_sib, lanes))
                here = pl.ds(s * PAIR + j * HEAD, HEAD)
                out = attended[:, here]
                inverse = lax.rsqrt(jnp.mean(out * out, axis=-1, keepdims=True) + epsilon)
                scaled = by_head[j] * gain[:, lanes]
                share = jnp.mean(scaled * out, axis=-1, keepdims=True)
                grad = (inverse * (scaled - out * (inverse * inverse * share))).astype(bf16)
                d_attended[:, here] = grad
                state[2 * chip + j] = dims(fq, grad, 0, 0).astype(bf16)


def inner_kernel(
    place, q_own, q_sib, k_own, k_sib, v_own, v_sib, near, far, d_attended, gq, part_k, part_v, sent
):
    half = q_own.shape[0]
    mask = causal_mask(place, 2 * half)
    mask_t = causal_mask(place, 2 * half, True)
    odd = lax.rem(place[0], 2) == 1
    for s in range(CHIPS):
        chip = chip_of(place, s)
        for j in range(2):
            lanes = head_lanes(place, chip, j)
            here = pl.ds(s * PAIR + j * HEAD, HEAD)
            there = pl.ds(pl.multiple_of(chip * PAIR + j * HEAD, HEAD), HEAD)
            query = rows_of(q_own, q_sib, lanes)
            fq = feature(query)
            fk = feature(rows_of(k_own, k_sib, lanes))
            value = rows_of(v_own, v_sib, lanes)
            grad = d_attended[:, here]
            prefix = entering_state(near, far, 2 * chip + j, odd)
            d_probs = jnp.where(mask, dims(grad, value, 1, 1), 0.0).astype(bf16)
            d_probs_t = jnp.where(mask_t, dims(value, grad, 1, 1), 0.0).astype(bf16)
            probs_t = jnp.where(mask_t, dims(fk, fq, 1, 1), 0.0).astype(bf16)
            d_fq = dims(d_probs, fk, 1, 0) + dims(grad, prefix, 1, 1)
            out = (d_fq * feature_slope(query)).astype(bf16)
            from_k = dims(d_probs_t, fq, 1, 0)
            from_v = dims(probs_t, grad, 1, 0)
            gq[:, lanes] = out[:half]
            part_k[:, there] = from_k[:half]
            part_v[:, there] = from_v[:half]
            sent[0, :, there] = out[half:]
            sent[1, :, there] = from_k[half:].astype(bf16)
            sent[2, :, there] = from_v[half:].astype(bf16)


def outer_kernel(place, k_own, v_own, near, near_sib, far, far_sib, part_k, part_v, got, gk, gv):
    odd = lax.rem(place[0], 2) == 1
    for chip in range(CHIPS):
        for j in range(2):
            there = pl.ds(chip * PAIR + j * HEAD, HEAD)
            for other in range(2):
                block = 2 * chip + (1 - place[1] if other else place[1])
                lanes = pl.ds(pl.multiple_of(block * PAIR + j * HEAD, HEAD), HEAD)
                states = (near_sib, far_sib) if other else (near, far)
                suffix = entering_state(*states, 2 * chip + j, jnp.logical_not(odd))
                from_k = got[1, :, there].astype(f32) if other else part_k[:, there]
                from_v = got[2, :, there].astype(f32) if other else part_v[:, there]
                key = k_own[:, lanes]
                d_fk = from_k + dims(v_own[:, lanes], suffix, 1, 1)
                gk[:, lanes] = (d_fk * feature_slope(key)).astype(bf16)
                gv[:, lanes] = (from_v + dims(feature(key), suffix, 1, 0)).astype(bf16)


def fill_kernel(place, got, held, out):
    for chip in range(CHIPS):
        pair = pl.ds(chip * PAIR, PAIR)
        own = pl.ds(pl.multiple_of((2 * chip + place[1]) * PAIR, PAIR), PAIR)
        other = pl.ds(pl.multiple_of((2 * chip + 1 - place[1]) * PAIR, PAIR), PAIR)
        out[:, own] = held[:, own]
        out[:, other] = got[0, :, pair]


def mixed_kernel(n0, n1, n2, n3, nx, w_own, w_sib, m0, m1, m2, m3):
    half = nx.shape[1]
    weight = jnp.concatenate([w_own[...], w_sib[...]], axis=0)
    for m, (n, out) in enumerate(zip((n0, n1, n2, n3), (m0, m1, m2, m3))):
        rows = jnp.concatenate([n[:half, :], nx[m]], axis=1)
        out[...] = dims(rows, weight, 1, 0).astype(out.dtype)


def weight_kernel(*refs):
    packs, cots, outs = refs[:COLUMNS], refs[COLUMNS : 3 * COLUMNS], refs[3 * COLUMNS :]
    half = cots[0].shape[0]
    total = None
    for m in range(COLUMNS):
        for part in range(2):
            term = dims(packs[m][pl.ds(part * half, half), :], cots[2 * m + part][...], 0, 0)
            total = term if total is None else total + term
    outs[0][...] = total[: 2 * QUARTER]
    outs[1][...] = total[2 * QUARTER :].astype(bf16)


def gathered_kernel(scale, place, t0, t1, t2, t3, out):
    for m, t in enumerate((t0, t1, t2, t3)):
        column = lax.bitwise_xor(place[2], m)
        out[pl.ds(pl.multiple_of(column * QUARTER, QUARTER), QUARTER), :] = t[...].astype(f32) * scale


def after(x, *earlier):
    return lax.optimization_barrier((x, *earlier))[0]


def on_device_planned(query_rows, key_rows, value_rows, norm_gain, out_weight, cotangent):
    query, key, value, cot = query_rows[0], key_rows[0], value_rows[0], cotangent[0]
    half, width = query.shape
    here, column = lax.axis_index("ctx"), lax.axis_index("dp")
    place = jnp.stack([here // 2, here % 2, column]).astype(jnp.int32)
    gain = norm_gain.reshape(1, width)
    heads = 2 * CHIPS
    state_shape = like((heads, HEAD, HEAD), bf16)
    state_flops = 2 * heads * 2 * half * HEAD * HEAD
    pack, full = like((2 * half, PAIR), bf16), like((half, width), bf16)
    part = like((half, width // 2), f32)
    step = 512

    def column_spec(rows, columns):
        return pl.BlockSpec((rows, columns), lambda i: (0, i))

    def fixed(shape):
        return pl.BlockSpec(shape, lambda i: (0,) * len(shape))

    def sent(x, name, axis, pairs):
        with jax.named_scope("send_" + name):
            return lax.ppermute(x, axis, pairs)

    def to_sib(x, name):
        return sent(x, name, "ctx", [(i, i ^ 1) for i in range(2 * CHIPS)])

    def swapped(x, s, name):
        pairs = [(2 * c + e, 2 * (c ^ s) + e) for c in range(CHIPS) for e in range(2)]
        return sent(x, name, "ctx", pairs)

    def halfway(x, s, name):
        pairs = [(2 * c + e, 2 * (c + s) + e) for c in range(CHIPS) for e in range(2) if 0 <= c + s < CHIPS]
        return sent(x, name, "ctx", pairs)

    def across(x, m, name):
        return sent(x, name, "dp", [(d, d ^ m) for d in range(COLUMNS)])

    key_sib = to_sib(key, "key")
    value_sib = to_sib(value, "value")
    state = call(
        states_kernel, [state_shape], "states", (place, key, key_sib, value, value_sib), state_flops
    )[0]
    query_sib = to_sib(after(query, state), "query")
    near = swapped(state, 1, "near")
    pair_state = state + near
    far = halfway(pair_state, 2, "far")
    sib0 = to_sib(after(cot, state), "sib0")
    attended, *packs = after(call(
        attend_kernel,
        [like((2 * half, heads * HEAD), f32)] + [pack] * COLUMNS,
        "attend",
        (place, query, query_sib, key, key_sib, value, value_sib, near, far, gain),
        8 * state_flops,
        hint=0,
    ), sib0)
    quarter = lax.dynamic_slice(out_weight, (column * QUARTER, 0), (QUARTER, width))
    w2 = swapped(quarter, 2, "w2")
    w_first = jnp.concatenate([quarter, w2], axis=0)
    w_second = swapped(w_first, 1, "w_second")
    cot1 = across(cot, 1, "cot1")
    sib1 = to_sib(cot1, "sib1")
    cot2 = across(cot, 2, "cot2")
    sib2 = to_sib(after(cot2, far), "sib2")
    cot3 = across(after(cot, cot2), 3, "cot3")
    sib3 = to_sib(cot3, "sib3")
    cot_parts = [cot, sib0, cot1, sib1, cot2, sib2, cot3, sib3]
    d_packs = call(
        d_normed_kernel,
        [pack] * COLUMNS,
        "d_normed",
        (w_first, w_second, *cot_parts),
        2 * 8 * half * PAIR * width,
    )
    n1 = after(across(packs[1], 1, "n1"), *d_packs)
    n2 = after(across(packs[2], 2, "n2"), *d_packs)
    n3 = after(across(packs[3], 3, "n3"), *d_packs)
    n_got = (packs[0], n1, n2, n3)
    kept, given = call(
        weight_kernel,
        [like((2 * QUARTER, width), f32), like((2 * QUARTER, width), bf16)],
        "weight_terms",
        (*n_got, *cot_parts),
        2 * 8 * half * PAIR * width,
        grid=(width // step,),
        in_specs=[fixed((2 * half, PAIR))] * COLUMNS + [column_spec(half, step)] * (2 * COLUMNS),
        out_specs=[column_spec(2 * QUARTER, step)] * 2,
    )
    n_sib = to_sib(after(jnp.stack([n[half:] for n in n_got]), given), "n_sib")
    weight = jnp.concatenate([w_first, w_second], axis=0)
    w_sib = to_sib(after(weight, given), "w_sib")
    outs = call(
        mixed_kernel,
        [like((half, width), f32)] + [like((half, width), bf16)] * (COLUMNS - 1),
        "mixed_terms",
        (*n_got, n_sib, weight, w_sib),
        2 * 4 * half * 2 * PAIR * width,
        grid=(width // step,),
        in_specs=[fixed((2 * half, PAIR))] * COLUMNS
        + [fixed((COLUMNS, half, PAIR))]
        + [column_spec(PAIR, step)] * 2,
        out_specs=[column_spec(half, step)] * COLUMNS,
    )
    mixed1 = across(outs[1], 1, "mixed1")
    mixed2 = across(outs[2], 2, "mixed2")
    mixed3 = across(outs[3], 3, "mixed3")
    mixed_got = [mixed1, mixed2, mixed3]
    mixed = outs[0]
    for x in mixed_got:
        mixed = mixed + x.astype(f32)
    mixed = mixed.astype(bf16)
    d1 = across(after(d_packs[1], given), 1, "d1")
    d2 = across(after(d_packs[2], given), 2, "d2")
    d3 = across(after(d_packs[3], given), 3, "d3")
    d_got = (d_packs[0], d1, d2, d3)
    d_attended, d_state = call(
        d_attend_kernel,
        [like((2 * half, heads * HEAD), bf16), state_shape],
        "d_attend",
        (place, query, query_sib, attended, gain, *d_got),
        2 * state_flops,
    )
    gq, part_k, part_v, parts_sent = call(
        inner_kernel,
        [full, part, part, like((3, half, width // 2), bf16)],
        "inner",
        (place, query, query_sib, key, key_sib, value, value_sib, near, far, after(d_attended, mixed)),
        14 * state_flops,
    )
    parts_got = to_sib(parts_sent, "parts")
    grad_queries = call(fill_kernel, [full], "fill_q", (place, parts_got, gq), 0)[0]
    terms = swapped(given, 1, "terms")
    d_near = swapped(after(d_state, terms), 1, "d_near")
    d_near_sib = to_sib(d_near, "d_near_sib")
    d_pair_state = d_state + d_near
    d_far = halfway(d_pair_state, -2, "d_far")
    d_far_sib = to_sib(d_far, "d_far_sib")
    grad_kv = call(
        outer_kernel,
        [full, full],
        "outer",
        (place, key, value, d_near, d_near_sib, d_far, d_far_sib, part_k, part_v, parts_got),
        2 * state_flops,
    )
    pair = kept + terms.astype(f32)
    pair_terms = after(swapped(pair[QUARTER:].astype(bf16), 2, "pair_terms"), gq)
    share = (pair[:QUARTER] + pair_terms.astype(f32)).astype(bf16)
    share1 = across(share, 1, "share1")
    share2 = across(share, 2, "share2")
    share3 = across(share, 3, "share3")
    scale = 1.0 / math.sqrt(lax.axis_size("dp") * lax.axis_size("ctx") * half)
    grad_weight = call(
        functools.partial(gathered_kernel, scale),
        [like(out_weight.shape, f32)],
        "grad_weight",
        (place, *(share, share1, share2, share3)),
        0,
    )[0]
    return (mixed[None], grad_queries[None], grad_kv[0][None], grad_kv[1][None], grad_weight)


def on_device(query_rows, key_rows, value_rows, norm_gain, out_weight, cotangent):
    fits = (
        lax.axis_size("dp") == COLUMNS
        and lax.axis_size("ctx") == 2 * CHIPS
        and out_weight.shape[0] == PAIR
        and out_weight.shape[1] == 2 * CHIPS * PAIR
        and query_rows.shape[1] == HEAD
    )
    path = on_device_planned if fits else on_device_general
    return path(query_rows, key_rows, value_rows, norm_gain, out_weight, cotangent)


def solution(mesh):
    return jax.shard_map(
        on_device,
        mesh=mesh,
        in_specs=(
            P("dp", "ctx", None),
            P("dp", "ctx", None),
            P("dp", "ctx", None),
            P(),
            P("ctx", None),
            P("dp", "ctx", None),
        ),
        out_specs=(
            P("dp", "ctx", None),
            P("dp", "ctx", None),
            P("dp", "ctx", None),
            P("dp", "ctx", None),
            P("ctx", None),
        ),
        check_vma=False,
    )
```

```python
import functools
import math

import jax
import jax.numpy as jnp
from jax import lax
from jax.experimental import pallas as pl
from jax.experimental.pallas import tpu as pltpu
from jax.sharding import PartitionSpec as P

HEAD = 128


epsilon = 1e-06
highest_precision = lax.Precision.HIGHEST


def carried_in(value, axis, combine, identity):
    size, index = (lax.axis_size(axis), lax.axis_index(axis))
    everything = lax.all_gather(value, axis)
    start = jnp.broadcast_to(jnp.asarray(identity, value.dtype), value.shape)

    def carried_turn(k, before):
        reached = k < index
        new = combine(before, everything[k])
        return jnp.where(reached, new, before)

    return lax.fori_loop(0, size, carried_turn, start)


def entering(value, axis, combine, identity):
    size, index = (lax.axis_size(axis), lax.axis_index(axis))
    everything = lax.all_gather(value.astype(jnp.bfloat16), axis)
    start = jnp.broadcast_to(jnp.asarray(identity, value.dtype), value.shape)

    def entering_turn(k, before):
        at = size - 1 - k
        reached = at > index
        new = combine(before, everything[at].astype(value.dtype))
        return jnp.where(reached, new, before)

    return lax.fori_loop(0, size, entering_turn, start)


def feature(values):
    wide = values.astype(jnp.float32)
    return jnp.where(wide > 0, wide + 1.0, jnp.exp(jnp.minimum(wide, 0.0))).astype(jnp.bfloat16)


def feature_slope(values):
    wide = values.astype(jnp.float32)
    return jnp.where(wide > 0, 1.0, jnp.exp(jnp.minimum(wide, 0.0)))


def add_states(earlier, later):
    return earlier + later


def on_device_general(query_rows, key_rows, value_rows, norm_gain, out_weight, cotangent):
    length = query_rows.shape[1]
    width = query_rows.shape[2]
    heads = width // HEAD
    shape3 = (length, heads, HEAD)
    weight = lax.all_gather(out_weight, "ctx", axis=0, tiled=True)
    query_seq = query_rows[0]
    key_seq = key_rows[0]
    query_per_head = feature(query_seq).reshape(shape3)
    key_per_head = feature(key_seq).reshape(shape3)
    value_per_head = value_rows[0].reshape(shape3)
    local_state = jnp.einsum(
        "wmx,wmt->mxt", key_per_head, value_per_head, preferred_element_type=jnp.float32
    )
    zero_state = jnp.zeros_like(local_state)
    prefix_state = carried_in(local_state, "ctx", add_states, zero_state)
    causal = jnp.tril(jnp.ones((length, length), dtype=bool))
    scores = jnp.einsum(
        "thd,shd->hts", query_per_head, key_per_head, preferred_element_type=jnp.float32
    )
    probs = jnp.where(causal, scores, 0.0).astype(jnp.bfloat16)
    query_wide_rows = query_per_head.astype(jnp.float32)
    attended_output = jnp.einsum(
        "hts,shv->thv", probs, value_per_head, preferred_element_type=jnp.float32
    )
    attended_output = attended_output + jnp.einsum(
        "wrf,rfp->wrp", query_wide_rows, prefix_state, precision=highest_precision
    )
    inverse = lax.rsqrt(
        jnp.mean(attended_output * attended_output, axis=-1, keepdims=True) + epsilon
    )
    gain_heads = norm_gain.reshape(heads, HEAD)
    normed = (attended_output * inverse * gain_heads).reshape(length, width).astype(jnp.bfloat16)
    mixed = jnp.dot(normed, weight, preferred_element_type=jnp.float32).astype(jnp.bfloat16)
    upstream = cotangent[0]
    d_normed = lax.dot_general(
        upstream, weight, (((1,), (1,)), ((), ())), preferred_element_type=jnp.float32
    ).reshape(shape3)
    scaled = d_normed * gain_heads
    attended_gradient = (
        inverse
        * (
            scaled
            - attended_output
            * inverse
            * inverse
            * jnp.mean(scaled * attended_output, axis=-1, keepdims=True)
        )
    ).astype(jnp.bfloat16)
    grad_local = jnp.einsum(
        "ibg,ibq->bgq", query_per_head, attended_gradient, preferred_element_type=jnp.float32
    )
    suffix_state = entering(grad_local, "ctx", add_states, zero_state)
    d_scores = jnp.einsum(
        "thv,shv->hts", attended_gradient, value_per_head, preferred_element_type=jnp.float32
    )
    d_probs = jnp.where(causal, d_scores, 0.0).astype(jnp.bfloat16)
    wide_gradient = attended_gradient.astype(jnp.float32)
    value_wide_rows = value_per_head.astype(jnp.float32)
    key_wide_rows = key_per_head.astype(jnp.float32)
    query_gradient = jnp.einsum(
        "hts,shk->thk", d_probs, key_per_head, preferred_element_type=jnp.float32
    )
    query_gradient = query_gradient + jnp.einsum(
        "fxn,xpn->fxp", wide_gradient, prefix_state, precision=highest_precision
    )
    key_gradient = jnp.einsum(
        "hts,thk->shk", d_probs, query_per_head, preferred_element_type=jnp.float32
    )
    key_gradient = key_gradient + jnp.einsum(
        "mcu,cxu->mcx", value_wide_rows, suffix_state, precision=highest_precision
    )
    value_gradient = jnp.einsum(
        "hts,thv->shv", probs, attended_gradient, preferred_element_type=jnp.float32
    )
    value_gradient = value_gradient + jnp.einsum(
        "inz,nzc->inc", key_wide_rows, suffix_state, precision=highest_precision
    )
    grad_queries = (query_gradient.reshape(length, width) * feature_slope(query_seq)).astype(
        jnp.bfloat16
    )
    grad_keys = (key_gradient.reshape(length, width) * feature_slope(key_seq)).astype(jnp.bfloat16)
    grad_values = value_gradient.reshape(length, width).astype(jnp.bfloat16)
    devices_dp = lax.axis_size("dp")
    devices_ctx = lax.axis_size("ctx")
    loss_scale = 1.0 / math.sqrt(devices_dp * devices_ctx * length)
    shares = lax.psum_scatter(
        lax.dot_general(
            normed, upstream, (((0,), (0,)), ((), ())), preferred_element_type=jnp.float32
        ).astype(jnp.bfloat16),
        "ctx",
        scatter_dimension=0,
        tiled=True,
    )
    summed = lax.psum(shares, "dp").astype(jnp.float32)
    grad_weight = summed * loss_scale
    return (mixed[None], grad_queries[None], grad_keys[None], grad_values[None], grad_weight)


CHIPS = 4
ORDER = (0, 2, 1, 3)
COLUMNS = 4
PAIR = 2 * HEAD
QUARTER = PAIR // COLUMNS
VMEM_LIMIT = 40 * 1024 * 1024
bf16 = jnp.bfloat16
f32 = jnp.float32


def dims(a, b, ca, cb):
    return lax.dot_general(a, b, (((ca,), (cb,)), ((), ())), preferred_element_type=f32)


def call(kernel, outs, name, args, flops, grid=(), in_specs=None, out_specs=None, scratch=(), hint=1):
    vmem = pl.BlockSpec(memory_space=pltpu.VMEM)
    smem = pl.BlockSpec(memory_space=pltpu.SMEM)
    if in_specs is None:
        in_specs = [smem if a.dtype == jnp.int32 else vmem for a in args]
    if out_specs is None:
        out_specs = [vmem for _ in outs]
    moved = sum(math.prod(a.shape) * a.dtype.itemsize for a in list(args) + list(outs))
    return pl.pallas_call(
        kernel,
        out_shape=list(outs),
        grid=grid,
        in_specs=in_specs,
        out_specs=out_specs,
        scratch_shapes=list(scratch),
        compiler_params=pltpu.CompilerParams(vmem_limit_bytes=VMEM_LIMIT),
        cost_estimate=pl.CostEstimate(flops=flops * hint, bytes_accessed=moved * hint, transcendentals=0),
        name=name,
    )(*args)


def like(shape, dtype):
    return jax.ShapeDtypeStruct(shape, dtype)


def chip_of(place, s):
    return lax.bitwise_xor(place[0], ORDER[s])


def head_lanes(place, chip, j):
    return pl.ds(pl.multiple_of((2 * chip + place[1]) * PAIR + j * HEAD, HEAD), HEAD)


def entering_state(near, far, at, takes_near):
    first = jnp.where(takes_near, near[at].astype(f32), 0.0)
    return (first + far[at].astype(f32)).astype(bf16)


def rows_of(own, sib, lanes):
    return jnp.concatenate([own[:, lanes], sib[:, lanes]], axis=0)


def causal_mask(place, rows, transposed=False):
    core = place[1]

    def position(axis):
        at = lax.broadcasted_iota(jnp.int32, (rows, rows), axis)
        half = rows // 2
        return jnp.where(at < half, at + core * half, at - core * half)

    query, key = (1, 0) if transposed else (0, 1)
    return position(key) <= position(query)


def states_kernel(place, k_own, k_sib, v_own, v_sib, state):
    for chip in range(CHIPS):
        for j in range(2):
            lanes = head_lanes(place, chip, j)
            fk = feature(rows_of(k_own, k_sib, lanes))
            state[2 * chip + j] = dims(fk, rows_of(v_own, v_sib, lanes), 0, 0).astype(bf16)


def attend_kernel(place, q_own, q_sib, k_own, k_sib, v_own, v_sib, near, far, gain, attended, n0, n1, n2, n3):
    rows = 2 * q_own.shape[0]
    mask = causal_mask(place, rows)
    odd = lax.rem(place[0], 2) == 1
    column = place[2]
    low = lax.broadcasted_iota(jnp.int32, (rows, HEAD), 1) < HEAD // 2
    turned = lax.rem(column, 2) == 1
    swapped = column >= 2
    packs = (n0, n1, n2, n3)
    for t in range(CHIPS // 2):
        pieces = []
        for s in (2 * t, 2 * t + 1):
            chip = chip_of(place, s)
            normed = []
            for j in range(2):
                lanes = head_lanes(place, chip, j)
                fq = feature(rows_of(q_own, q_sib, lanes))
                fk = feature(rows_of(k_own, k_sib, lanes))
                value = rows_of(v_own, v_sib, lanes)
                probs = jnp.where(mask, dims(fq, fk, 1, 1), 0.0).astype(bf16)
                prefix = entering_state(near, far, 2 * chip + j, odd)
                out = dims(probs, value, 1, 0) + dims(fq, prefix, 1, 0)
                attended[:, pl.ds(s * PAIR + j * HEAD, HEAD)] = out
                inverse = lax.rsqrt(jnp.mean(out * out, axis=-1, keepdims=True) + epsilon)
                normed.append(out * inverse * gain[:, lanes])
            first = jnp.where(swapped, normed[1], normed[0])
            second = jnp.where(swapped, normed[0], normed[1])
            pieces.append([jnp.where(turned, pltpu.roll(x, HEAD // 2, 1), x) for x in (first, second)])
        for i in range(2):
            a, b = pieces[0][i], pieces[1][i]
            at = pl.ds(t * HEAD, HEAD)
            packs[2 * i][:, at] = jnp.where(low, a, pltpu.roll(b, HEAD // 2, 1)).astype(bf16)
            packs[2 * i + 1][:, at] = jnp.where(low, pltpu.roll(a, HEAD // 2, 1), b).astype(bf16)


def d_normed_kernel(w_first, w_second, *refs):
    cots, outs = refs[: 2 * COLUMNS], refs[2 * COLUMNS :]
    half = cots[0].shape[0]
    weight = jnp.concatenate([w_first[...], w_second[...]], axis=0)
    for m in range(COLUMNS):
        outs[m][:half] = dims(cots[2 * m][...], weight, 1, 1).astype(bf16)
        outs[m][half:] = dims(cots[2 * m + 1][...], weight, 1, 1).astype(bf16)


def d_attend_kernel(place, q_own, q_sib, attended, gain, r0, r1, r2, r3, d_attended, state):
    rows = 2 * q_own.shape[0]
    column = place[2]
    low = lax.broadcasted_iota(jnp.int32, (rows, HEAD), 1) < HEAD // 2
    turned = lax.rem(column, 2) == 1
    swapped = column >= 2
    packs = (r0, r1, r2, r3)
    for t in range(CHIPS // 2):
        at = pl.ds(t * HEAD, HEAD)
        pieces = [[], []]
        for i in range(2):
            a, b = packs[2 * i][:, at].astype(f32), packs[2 * i + 1][:, at].astype(f32)
            both = (
                jnp.where(low, a, pltpu.roll(b, HEAD // 2, 1)),
                jnp.where(low, pltpu.roll(a, HEAD // 2, 1), b),
            )
            for which in range(2):
                x = both[which]
                pieces[which].append(jnp.where(turned, pltpu.roll(x, HEAD // 2, 1), x))
        for which in range(2):
            s = 2 * t + which
            chip = chip_of(place, s)
            first, second = pieces[which]
            by_head = (jnp.where(swapped, second, first), jnp.where(swapped, first, second))
            for j in range(2):
                lanes = head_lanes(place, chip, j)
                fq = feature(rows_of(q_own, q_sib, lanes))
                here = pl.ds(s * PAIR + j * HEAD, HEAD)
                out = attended[:, here]
                inverse = lax.rsqrt(jnp.mean(out * out, axis=-1, keepdims=True) + epsilon)
                scaled = by_head[j] * gain[:, lanes]
                share = jnp.mean(scaled * out, axis=-1, keepdims=True)
                grad = (inverse * (scaled - out * (inverse * inverse * share))).astype(bf16)
                d_attended[:, here] = grad
                state[2 * chip + j] = dims(fq, grad, 0, 0).astype(bf16)


def inner_kernel(
    place, q_own, q_sib, k_own, k_sib, v_own, v_sib, near, far, d_attended, gq, part_k, part_v, sent
):
    half = q_own.shape[0]
    mask = causal_mask(place, 2 * half)
    mask_t = causal_mask(place, 2 * half, True)
    odd = lax.rem(place[0], 2) == 1
    for s in range(CHIPS):
        chip = chip_of(place, s)
        for j in range(2):
            lanes = head_lanes(place, chip, j)
            here = pl.ds(s * PAIR + j * HEAD, HEAD)
            there = pl.ds(pl.multiple_of(chip * PAIR + j * HEAD, HEAD), HEAD)
            query = rows_of(q_own, q_sib, lanes)
            fq = feature(query)
            fk = feature(rows_of(k_own, k_sib, lanes))
            value = rows_of(v_own, v_sib, lanes)
            grad = d_attended[:, here]
            prefix = entering_state(near, far, 2 * chip + j, odd)
            d_probs = jnp.where(mask, dims(grad, value, 1, 1), 0.0).astype(bf16)
            d_probs_t = jnp.where(mask_t, dims(value, grad, 1, 1), 0.0).astype(bf16)
            probs_t = jnp.where(mask_t, dims(fk, fq, 1, 1), 0.0).astype(bf16)
            d_fq = dims(d_probs, fk, 1, 0) + dims(grad, prefix, 1, 1)
            out = (d_fq * feature_slope(query)).astype(bf16)
            from_k = dims(d_probs_t, fq, 1, 0)
            from_v = dims(probs_t, grad, 1, 0)
            gq[:, lanes] = out[:half]
            part_k[:, there] = from_k[:half]
            part_v[:, there] = from_v[:half]
            sent[0, :, there] = out[half:]
            sent[1, :, there] = from_k[half:].astype(bf16)
            sent[2, :, there] = from_v[half:].astype(bf16)


def outer_kernel(place, k_own, v_own, near, near_sib, far, far_sib, part_k, part_v, got, gk, gv):
    odd = lax.rem(place[0], 2) == 1
    for chip in range(CHIPS):
        for j in range(2):
            there = pl.ds(chip * PAIR + j * HEAD, HEAD)
            for other in range(2):
                block = 2 * chip + (1 - place[1] if other else place[1])
                lanes = pl.ds(pl.multiple_of(block * PAIR + j * HEAD, HEAD), HEAD)
                states = (near_sib, far_sib) if other else (near, far)
                suffix = entering_state(*states, 2 * chip + j, jnp.logical_not(odd))
                from_k = got[1, :, there].astype(f32) if other else part_k[:, there]
                from_v = got[2, :, there].astype(f32) if other else part_v[:, there]
                key = k_own[:, lanes]
                d_fk = from_k + dims(v_own[:, lanes], suffix, 1, 1)
                gk[:, lanes] = (d_fk * feature_slope(key)).astype(bf16)
                gv[:, lanes] = (from_v + dims(feature(key), suffix, 1, 0)).astype(bf16)


def fill_kernel(place, got, held, out):
    for chip in range(CHIPS):
        pair = pl.ds(chip * PAIR, PAIR)
        own = pl.ds(pl.multiple_of((2 * chip + place[1]) * PAIR, PAIR), PAIR)
        other = pl.ds(pl.multiple_of((2 * chip + 1 - place[1]) * PAIR, PAIR), PAIR)
        out[:, own] = held[:, own]
        out[:, other] = got[0, :, pair]


def mixed_kernel(n0, n1, n2, n3, nx, w_own, w_sib, m0, m1, m2, m3):
    half = nx.shape[1]
    weight = jnp.concatenate([w_own[...], w_sib[...]], axis=0)
    for m, (n, out) in enumerate(zip((n0, n1, n2, n3), (m0, m1, m2, m3))):
        rows = jnp.concatenate([n[:half, :], nx[m]], axis=1)
        out[...] = dims(rows, weight, 1, 0).astype(out.dtype)


def weight_kernel(*refs):
    packs, cots, outs = refs[:COLUMNS], refs[COLUMNS : 3 * COLUMNS], refs[3 * COLUMNS :]
    half = cots[0].shape[0]
    total = None
    for m in range(COLUMNS):
        for part in range(2):
            term = dims(packs[m][pl.ds(part * half, half), :], cots[2 * m + part][...], 0, 0)
            total = term if total is None else total + term
    outs[0][...] = total[: 2 * QUARTER]
    outs[1][...] = total[2 * QUARTER :].astype(bf16)


def gathered_kernel(scale, place, t0, t1, t2, t3, out):
    for m, t in enumerate((t0, t1, t2, t3)):
        column = lax.bitwise_xor(place[2], m)
        out[pl.ds(pl.multiple_of(column * QUARTER, QUARTER), QUARTER), :] = t[...].astype(f32) * scale


def finish_kernel(place, got, held, k_own, v_own, near, near_sib, far, far_sib, part_k, part_v, gq, gk, gv):
    fill_kernel(place, got, held, gq)
    outer_kernel(place, k_own, v_own, near, near_sib, far, far_sib, part_k, part_v, got, gk, gv)


def after(x, *earlier):
    return lax.optimization_barrier((x, *earlier))[0]


def on_device_planned(query_rows, key_rows, value_rows, norm_gain, out_weight, cotangent):
    query, key, value, cot = query_rows[0], key_rows[0], value_rows[0], cotangent[0]
    half, width = query.shape
    here, column = lax.axis_index("ctx"), lax.axis_index("dp")
    place = jnp.stack([here // 2, here % 2, column]).astype(jnp.int32)
    gain = norm_gain.reshape(1, width)
    heads = 2 * CHIPS
    state_shape = like((heads, HEAD, HEAD), bf16)
    state_flops = 2 * heads * 2 * half * HEAD * HEAD
    pack, full = like((2 * half, PAIR), bf16), like((half, width), bf16)
    part = like((half, width // 2), f32)
    step = 512

    def column_spec(rows, columns):
        return pl.BlockSpec((rows, columns), lambda i: (0, i))

    def fixed(shape):
        return pl.BlockSpec(shape, lambda i: (0,) * len(shape))

    def sent(x, name, axis, pairs):
        with jax.named_scope("send_" + name):
            return lax.ppermute(x, axis, pairs)

    def to_sib(x, name):
        return sent(x, name, "ctx", [(i, i ^ 1) for i in range(2 * CHIPS)])

    def swapped(x, s, name):
        pairs = [(2 * c + e, 2 * (c ^ s) + e) for c in range(CHIPS) for e in range(2)]
        return sent(x, name, "ctx", pairs)

    def halfway(x, s, name):
        pairs = [(2 * c + e, 2 * (c + s) + e) for c in range(CHIPS) for e in range(2) if 0 <= c + s < CHIPS]
        return sent(x, name, "ctx", pairs)

    def across(x, m, name):
        return sent(x, name, "dp", [(d, d ^ m) for d in range(COLUMNS)])

    key_sib = to_sib(key, "key")
    value_sib = to_sib(value, "value")
    state = call(
        states_kernel, [state_shape], "states", (place, key, key_sib, value, value_sib), state_flops
    )[0]
    query_sib = to_sib(after(query, state), "query")
    near = swapped(state, 1, "near")
    pair_state = state + near
    far = halfway(pair_state, 2, "far")
    sib0 = to_sib(after(cot, state), "sib0")
    attended, *packs = after(call(
        attend_kernel,
        [like((2 * half, heads * HEAD), f32)] + [pack] * COLUMNS,
        "attend",
        (place, query, query_sib, key, key_sib, value, value_sib, near, far, gain),
        8 * state_flops,
        hint=0,
    ), sib0)
    quarter = lax.dynamic_slice(out_weight, (column * QUARTER, 0), (QUARTER, width))
    w2 = swapped(quarter, 2, "w2")
    w_first = jnp.concatenate([quarter, w2], axis=0)
    w_second = swapped(w_first, 1, "w_second")
    cot1 = across(cot, 1, "cot1")
    sib1 = to_sib(cot1, "sib1")
    cot2 = across(cot, 2, "cot2")
    sib2 = to_sib(after(cot2, far), "sib2")
    cot3 = across(after(cot, cot2), 3, "cot3")
    sib3 = to_sib(cot3, "sib3")
    cot_parts = [cot, sib0, cot1, sib1, cot2, sib2, cot3, sib3]
    d_packs = call(
        d_normed_kernel,
        [pack] * COLUMNS,
        "d_normed",
        (w_first, w_second, *cot_parts),
        2 * 8 * half * PAIR * width,
    )
    n1 = after(across(packs[1], 1, "n1"), *d_packs)
    n2 = after(across(packs[2], 2, "n2"), *d_packs)
    n3 = after(across(packs[3], 3, "n3"), *d_packs)
    n_got = (packs[0], n1, n2, n3)
    kept, given = call(
        weight_kernel,
        [like((2 * QUARTER, width), f32), like((2 * QUARTER, width), bf16)],
        "weight_terms",
        (*n_got, *cot_parts),
        2 * 8 * half * PAIR * width,
        grid=(width // step,),
        in_specs=[fixed((2 * half, PAIR))] * COLUMNS + [column_spec(half, step)] * (2 * COLUMNS),
        out_specs=[column_spec(2 * QUARTER, step)] * 2,
    )
    n_sib = to_sib(after(jnp.stack([n[half:] for n in n_got]), given), "n_sib")
    weight = jnp.concatenate([w_first, w_second], axis=0)
    w_sib = to_sib(after(weight, given), "w_sib")
    outs = call(
        mixed_kernel,
        [like((half, width), f32)] + [like((half, width), bf16)] * (COLUMNS - 1),
        "mixed_terms",
        (*n_got, n_sib, weight, w_sib),
        2 * 4 * half * 2 * PAIR * width,
        grid=(width // step,),
        in_specs=[fixed((2 * half, PAIR))] * COLUMNS
        + [fixed((COLUMNS, half, PAIR))]
        + [column_spec(PAIR, step)] * 2,
        out_specs=[column_spec(half, step)] * COLUMNS,
    )
    mixed1 = across(outs[1], 1, "mixed1")
    mixed2 = across(outs[2], 2, "mixed2")
    mixed3 = across(outs[3], 3, "mixed3")
    mixed_got = [mixed1, mixed2, mixed3]
    mixed = outs[0]
    for x in mixed_got:
        mixed = mixed + x.astype(f32)
    mixed = mixed.astype(bf16)
    d1 = across(after(d_packs[1], given), 1, "d1")
    d2 = across(after(d_packs[2], given), 2, "d2")
    d3 = across(after(d_packs[3], given), 3, "d3")
    d_got = (d_packs[0], d1, d2, d3)
    d_attended, d_state = call(
        d_attend_kernel,
        [like((2 * half, heads * HEAD), bf16), state_shape],
        "d_attend",
        (place, query, query_sib, attended, gain, *d_got),
        2 * state_flops,
    )
    gq, part_k, part_v, parts_sent = call(
        inner_kernel,
        [full, part, part, like((3, half, width // 2), bf16)],
        "inner",
        (place, query, query_sib, key, key_sib, value, value_sib, near, far, after(d_attended, mixed)),
        14 * state_flops,
    )
    parts_got = to_sib(parts_sent, "parts")
    terms = swapped(given, 1, "terms")
    d_near = swapped(after(d_state, terms), 1, "d_near")
    d_near_sib = to_sib(d_near, "d_near_sib")
    d_pair_state = d_state + d_near
    d_far = halfway(d_pair_state, -2, "d_far")
    d_far_sib = to_sib(d_far, "d_far_sib")
    pair = kept + terms.astype(f32)
    pair_terms = after(swapped(pair[QUARTER:].astype(bf16), 2, "pair_terms"), gq)
    share = (pair[:QUARTER] + pair_terms.astype(f32)).astype(bf16)
    share1 = across(share, 1, "share1")
    share2 = across(share, 2, "share2")
    share3 = across(share, 3, "share3")
    scale = 1.0 / math.sqrt(lax.axis_size("dp") * lax.axis_size("ctx") * half)
    grad_queries, *grad_kv = call(
        finish_kernel,
        [full, full, full],
        "finish",
        (place, parts_got, gq, key, value, d_near, d_near_sib, d_far, d_far_sib, part_k, part_v),
        2 * state_flops,
    )
    grad_weight = call(
        functools.partial(gathered_kernel, scale),
        [like(out_weight.shape, f32)],
        "grad_weight",
        (place, *(share, share1, share2, share3)),
        0,
    )[0]
    return (mixed[None], grad_queries[None], grad_kv[0][None], grad_kv[1][None], grad_weight)


def on_device(query_rows, key_rows, value_rows, norm_gain, out_weight, cotangent):
    fits = (
        lax.axis_size("dp") == COLUMNS
        and lax.axis_size("ctx") == 2 * CHIPS
        and out_weight.shape[0] == PAIR
        and out_weight.shape[1] == 2 * CHIPS * PAIR
        and query_rows.shape[1] == HEAD
    )
    path = on_device_planned if fits else on_device_general
    return path(query_rows, key_rows, value_rows, norm_gain, out_weight, cotangent)


def solution(mesh):
    return jax.shard_map(
        on_device,
        mesh=mesh,
        in_specs=(
            P("dp", "ctx", None),
            P("dp", "ctx", None),
            P("dp", "ctx", None),
            P(),
            P("ctx", None),
            P("dp", "ctx", None),
        ),
        out_specs=(
            P("dp", "ctx", None),
            P("dp", "ctx", None),
            P("dp", "ctx", None),
            P("dp", "ctx", None),
            P("ctx", None),
        ),
        check_vma=False,
    )
```

```python
import functools
import math

import jax
import jax.numpy as jnp
from jax import lax
from jax.experimental import pallas as pl
from jax.experimental.pallas import tpu as pltpu
from jax.sharding import PartitionSpec as P

HEAD = 128


epsilon = 1e-06
highest_precision = lax.Precision.HIGHEST


def carried_in(value, axis, combine, identity):
    size, index = (lax.axis_size(axis), lax.axis_index(axis))
    everything = lax.all_gather(value, axis)
    start = jnp.broadcast_to(jnp.asarray(identity, value.dtype), value.shape)

    def carried_turn(k, before):
        reached = k < index
        new = combine(before, everything[k])
        return jnp.where(reached, new, before)

    return lax.fori_loop(0, size, carried_turn, start)


def entering(value, axis, combine, identity):
    size, index = (lax.axis_size(axis), lax.axis_index(axis))
    everything = lax.all_gather(value.astype(jnp.bfloat16), axis)
    start = jnp.broadcast_to(jnp.asarray(identity, value.dtype), value.shape)

    def entering_turn(k, before):
        at = size - 1 - k
        reached = at > index
        new = combine(before, everything[at].astype(value.dtype))
        return jnp.where(reached, new, before)

    return lax.fori_loop(0, size, entering_turn, start)


def feature(values):
    wide = values.astype(jnp.float32)
    return jnp.where(wide > 0, wide + 1.0, jnp.exp(jnp.minimum(wide, 0.0))).astype(jnp.bfloat16)


def feature_slope(values):
    wide = values.astype(jnp.float32)
    return jnp.where(wide > 0, 1.0, jnp.exp(jnp.minimum(wide, 0.0)))


def add_states(earlier, later):
    return earlier + later


def on_device_general(query_rows, key_rows, value_rows, norm_gain, out_weight, cotangent):
    length = query_rows.shape[1]
    width = query_rows.shape[2]
    heads = width // HEAD
    shape3 = (length, heads, HEAD)
    weight = lax.all_gather(out_weight, "ctx", axis=0, tiled=True)
    query_seq = query_rows[0]
    key_seq = key_rows[0]
    query_per_head = feature(query_seq).reshape(shape3)
    key_per_head = feature(key_seq).reshape(shape3)
    value_per_head = value_rows[0].reshape(shape3)
    local_state = jnp.einsum(
        "wmx,wmt->mxt", key_per_head, value_per_head, preferred_element_type=jnp.float32
    )
    zero_state = jnp.zeros_like(local_state)
    prefix_state = carried_in(local_state, "ctx", add_states, zero_state)
    causal = jnp.tril(jnp.ones((length, length), dtype=bool))
    scores = jnp.einsum(
        "thd,shd->hts", query_per_head, key_per_head, preferred_element_type=jnp.float32
    )
    probs = jnp.where(causal, scores, 0.0).astype(jnp.bfloat16)
    query_wide_rows = query_per_head.astype(jnp.float32)
    attended_output = jnp.einsum(
        "hts,shv->thv", probs, value_per_head, preferred_element_type=jnp.float32
    )
    attended_output = attended_output + jnp.einsum(
        "wrf,rfp->wrp", query_wide_rows, prefix_state, precision=highest_precision
    )
    inverse = lax.rsqrt(
        jnp.mean(attended_output * attended_output, axis=-1, keepdims=True) + epsilon
    )
    gain_heads = norm_gain.reshape(heads, HEAD)
    normed = (attended_output * inverse * gain_heads).reshape(length, width).astype(jnp.bfloat16)
    mixed = jnp.dot(normed, weight, preferred_element_type=jnp.float32).astype(jnp.bfloat16)
    upstream = cotangent[0]
    d_normed = lax.dot_general(
        upstream, weight, (((1,), (1,)), ((), ())), preferred_element_type=jnp.float32
    ).reshape(shape3)
    scaled = d_normed * gain_heads
    attended_gradient = (
        inverse
        * (
            scaled
            - attended_output
            * inverse
            * inverse
            * jnp.mean(scaled * attended_output, axis=-1, keepdims=True)
        )
    ).astype(jnp.bfloat16)
    grad_local = jnp.einsum(
        "ibg,ibq->bgq", query_per_head, attended_gradient, preferred_element_type=jnp.float32
    )
    suffix_state = entering(grad_local, "ctx", add_states, zero_state)
    d_scores = jnp.einsum(
        "thv,shv->hts", attended_gradient, value_per_head, preferred_element_type=jnp.float32
    )
    d_probs = jnp.where(causal, d_scores, 0.0).astype(jnp.bfloat16)
    wide_gradient = attended_gradient.astype(jnp.float32)
    value_wide_rows = value_per_head.astype(jnp.float32)
    key_wide_rows = key_per_head.astype(jnp.float32)
    query_gradient = jnp.einsum(
        "hts,shk->thk", d_probs, key_per_head, preferred_element_type=jnp.float32
    )
    query_gradient = query_gradient + jnp.einsum(
        "fxn,xpn->fxp", wide_gradient, prefix_state, precision=highest_precision
    )
    key_gradient = jnp.einsum(
        "hts,thk->shk", d_probs, query_per_head, preferred_element_type=jnp.float32
    )
    key_gradient = key_gradient + jnp.einsum(
        "mcu,cxu->mcx", value_wide_rows, suffix_state, precision=highest_precision
    )
    value_gradient = jnp.einsum(
        "hts,thv->shv", probs, attended_gradient, preferred_element_type=jnp.float32
    )
    value_gradient = value_gradient + jnp.einsum(
        "inz,nzc->inc", key_wide_rows, suffix_state, precision=highest_precision
    )
    grad_queries = (query_gradient.reshape(length, width) * feature_slope(query_seq)).astype(
        jnp.bfloat16
    )
    grad_keys = (key_gradient.reshape(length, width) * feature_slope(key_seq)).astype(jnp.bfloat16)
    grad_values = value_gradient.reshape(length, width).astype(jnp.bfloat16)
    devices_dp = lax.axis_size("dp")
    devices_ctx = lax.axis_size("ctx")
    loss_scale = 1.0 / math.sqrt(devices_dp * devices_ctx * length)
    shares = lax.psum_scatter(
        lax.dot_general(
            normed, upstream, (((0,), (0,)), ((), ())), preferred_element_type=jnp.float32
        ).astype(jnp.bfloat16),
        "ctx",
        scatter_dimension=0,
        tiled=True,
    )
    summed = lax.psum(shares, "dp").astype(jnp.float32)
    grad_weight = summed * loss_scale
    return (mixed[None], grad_queries[None], grad_keys[None], grad_values[None], grad_weight)


CHIPS = 4
ORDER = (0, 2, 1, 3)
COLUMNS = 4
PAIR = 2 * HEAD
QUARTER = PAIR // COLUMNS
VMEM_LIMIT = 40 * 1024 * 1024
bf16 = jnp.bfloat16
f32 = jnp.float32


def dims(a, b, ca, cb):
    return lax.dot_general(a, b, (((ca,), (cb,)), ((), ())), preferred_element_type=f32)


def call(kernel, outs, name, args, flops, grid=(), in_specs=None, out_specs=None, scratch=(), hint=1):
    vmem = pl.BlockSpec(memory_space=pltpu.VMEM)
    smem = pl.BlockSpec(memory_space=pltpu.SMEM)
    if in_specs is None:
        in_specs = [smem if a.dtype == jnp.int32 else vmem for a in args]
    if out_specs is None:
        out_specs = [vmem for _ in outs]
    moved = sum(math.prod(a.shape) * a.dtype.itemsize for a in list(args) + list(outs))
    return pl.pallas_call(
        kernel,
        out_shape=list(outs),
        grid=grid,
        in_specs=in_specs,
        out_specs=out_specs,
        scratch_shapes=list(scratch),
        compiler_params=pltpu.CompilerParams(vmem_limit_bytes=VMEM_LIMIT),
        cost_estimate=pl.CostEstimate(flops=flops * hint, bytes_accessed=moved * hint, transcendentals=0),
        name=name,
    )(*args)


def like(shape, dtype):
    return jax.ShapeDtypeStruct(shape, dtype)


def chip_of(place, s):
    return lax.bitwise_xor(place[0], ORDER[s])


def head_lanes(place, chip, j):
    return pl.ds(pl.multiple_of((2 * chip + place[1]) * PAIR + j * HEAD, HEAD), HEAD)


def entering_state(near, far, at, takes_near):
    first = jnp.where(takes_near, near[at].astype(f32), 0.0)
    return (first + far[at].astype(f32)).astype(bf16)


def rows_of(own, sib, lanes):
    return jnp.concatenate([own[:, lanes], sib[:, lanes]], axis=0)


def causal_mask(place, rows, transposed=False):
    core = place[1]

    def position(axis):
        at = lax.broadcasted_iota(jnp.int32, (rows, rows), axis)
        half = rows // 2
        return jnp.where(at < half, at + core * half, at - core * half)

    query, key = (1, 0) if transposed else (0, 1)
    return position(key) <= position(query)


def states_kernel(place, k_own, k_sib, v_own, v_sib, state):
    for chip in range(CHIPS):
        for j in range(2):
            lanes = head_lanes(place, chip, j)
            fk = feature(rows_of(k_own, k_sib, lanes))
            state[2 * chip + j] = dims(fk, rows_of(v_own, v_sib, lanes), 0, 0).astype(bf16)


def attend_kernel(place, q_own, q_sib, k_own, k_sib, v_own, v_sib, near, far, gain, attended, n0, n1, n2, n3):
    rows = 2 * q_own.shape[0]
    mask = causal_mask(place, rows)
    odd = lax.rem(place[0], 2) == 1
    column = place[2]
    low = lax.broadcasted_iota(jnp.int32, (rows, HEAD), 1) < HEAD // 2
    turned = lax.rem(column, 2) == 1
    swapped = column >= 2
    packs = (n0, n1, n2, n3)
    for t in range(CHIPS // 2):
        pieces = []
        for s in (2 * t, 2 * t + 1):
            chip = chip_of(place, s)
            normed = []
            for j in range(2):
                lanes = head_lanes(place, chip, j)
                fq = feature(rows_of(q_own, q_sib, lanes))
                fk = feature(rows_of(k_own, k_sib, lanes))
                value = rows_of(v_own, v_sib, lanes)
                probs = jnp.where(mask, dims(fq, fk, 1, 1), 0.0).astype(bf16)
                prefix = entering_state(near, far, 2 * chip + j, odd)
                out = dims(probs, value, 1, 0) + dims(fq, prefix, 1, 0)
                attended[:, pl.ds(s * PAIR + j * HEAD, HEAD)] = out
                inverse = lax.rsqrt(jnp.mean(out * out, axis=-1, keepdims=True) + epsilon)
                normed.append(out * inverse * gain[:, lanes])
            first = jnp.where(swapped, normed[1], normed[0])
            second = jnp.where(swapped, normed[0], normed[1])
            pieces.append([jnp.where(turned, pltpu.roll(x, HEAD // 2, 1), x) for x in (first, second)])
        for i in range(2):
            a, b = pieces[0][i], pieces[1][i]
            at = pl.ds(t * HEAD, HEAD)
            packs[2 * i][:, at] = jnp.where(low, a, pltpu.roll(b, HEAD // 2, 1)).astype(bf16)
            packs[2 * i + 1][:, at] = jnp.where(low, pltpu.roll(a, HEAD // 2, 1), b).astype(bf16)


def d_normed_kernel(w_first, w_second, *refs):
    cots, outs = refs[: 2 * COLUMNS], refs[2 * COLUMNS :]
    half = cots[0].shape[0]
    weight = jnp.concatenate([w_first[...], w_second[...]], axis=0)
    for m in range(COLUMNS):
        outs[m][:half] = dims(cots[2 * m][...], weight, 1, 1).astype(bf16)
        outs[m][half:] = dims(cots[2 * m + 1][...], weight, 1, 1).astype(bf16)


def d_attend_kernel(place, q_own, q_sib, attended, gain, r0, r1, r2, r3, d_attended, state):
    rows = 2 * q_own.shape[0]
    column = place[2]
    low = lax.broadcasted_iota(jnp.int32, (rows, HEAD), 1) < HEAD // 2
    turned = lax.rem(column, 2) == 1
    swapped = column >= 2
    packs = (r0, r1, r2, r3)
    for t in range(CHIPS // 2):
        at = pl.ds(t * HEAD, HEAD)
        pieces = [[], []]
        for i in range(2):
            a, b = packs[2 * i][:, at].astype(f32), packs[2 * i + 1][:, at].astype(f32)
            both = (
                jnp.where(low, a, pltpu.roll(b, HEAD // 2, 1)),
                jnp.where(low, pltpu.roll(a, HEAD // 2, 1), b),
            )
            for which in range(2):
                x = both[which]
                pieces[which].append(jnp.where(turned, pltpu.roll(x, HEAD // 2, 1), x))
        for which in range(2):
            s = 2 * t + which
            chip = chip_of(place, s)
            first, second = pieces[which]
            by_head = (jnp.where(swapped, second, first), jnp.where(swapped, first, second))
            for j in range(2):
                lanes = head_lanes(place, chip, j)
                fq = feature(rows_of(q_own, q_sib, lanes))
                here = pl.ds(s * PAIR + j * HEAD, HEAD)
                out = attended[:, here]
                inverse = lax.rsqrt(jnp.mean(out * out, axis=-1, keepdims=True) + epsilon)
                scaled = by_head[j] * gain[:, lanes]
                share = jnp.mean(scaled * out, axis=-1, keepdims=True)
                grad = (inverse * (scaled - out * (inverse * inverse * share))).astype(bf16)
                d_attended[:, here] = grad
                state[2 * chip + j] = dims(fq, grad, 0, 0).astype(bf16)


def inner_kernel(
    place, q_own, q_sib, k_own, k_sib, v_own, v_sib, near, far, d_attended, gq, part_k, part_v, sent
):
    half = q_own.shape[0]
    mask = causal_mask(place, 2 * half)
    mask_t = causal_mask(place, 2 * half, True)
    odd = lax.rem(place[0], 2) == 1
    for s in range(CHIPS):
        chip = chip_of(place, s)
        for j in range(2):
            lanes = head_lanes(place, chip, j)
            here = pl.ds(s * PAIR + j * HEAD, HEAD)
            there = pl.ds(pl.multiple_of(chip * PAIR + j * HEAD, HEAD), HEAD)
            query = rows_of(q_own, q_sib, lanes)
            fq = feature(query)
            fk = feature(rows_of(k_own, k_sib, lanes))
            value = rows_of(v_own, v_sib, lanes)
            grad = d_attended[:, here]
            prefix = entering_state(near, far, 2 * chip + j, odd)
            d_probs = jnp.where(mask, dims(grad, value, 1, 1), 0.0).astype(bf16)
            d_probs_t = jnp.where(mask_t, dims(value, grad, 1, 1), 0.0).astype(bf16)
            probs_t = jnp.where(mask_t, dims(fk, fq, 1, 1), 0.0).astype(bf16)
            d_fq = dims(d_probs, fk, 1, 0) + dims(grad, prefix, 1, 1)
            out = (d_fq * feature_slope(query)).astype(bf16)
            from_k = dims(d_probs_t, fq, 1, 0)
            from_v = dims(probs_t, grad, 1, 0)
            gq[:, lanes] = out[:half]
            part_k[:, there] = from_k[:half]
            part_v[:, there] = from_v[:half]
            sent[0, :, there] = out[half:]
            sent[1, :, there] = from_k[half:].astype(bf16)
            sent[2, :, there] = from_v[half:].astype(bf16)


def outer_kernel(place, k_own, v_own, near, near_sib, far, far_sib, part_k, part_v, got, gk, gv):
    odd = lax.rem(place[0], 2) == 1
    for chip in range(CHIPS):
        for j in range(2):
            there = pl.ds(chip * PAIR + j * HEAD, HEAD)
            for other in range(2):
                block = 2 * chip + (1 - place[1] if other else place[1])
                lanes = pl.ds(pl.multiple_of(block * PAIR + j * HEAD, HEAD), HEAD)
                states = (near_sib, far_sib) if other else (near, far)
                suffix = entering_state(*states, 2 * chip + j, jnp.logical_not(odd))
                from_k = got[1, :, there].astype(f32) if other else part_k[:, there]
                from_v = got[2, :, there].astype(f32) if other else part_v[:, there]
                key = k_own[:, lanes]
                d_fk = from_k + dims(v_own[:, lanes], suffix, 1, 1)
                gk[:, lanes] = (d_fk * feature_slope(key)).astype(bf16)
                gv[:, lanes] = (from_v + dims(feature(key), suffix, 1, 0)).astype(bf16)


def fill_kernel(place, got, held, out):
    for chip in range(CHIPS):
        pair = pl.ds(chip * PAIR, PAIR)
        own = pl.ds(pl.multiple_of((2 * chip + place[1]) * PAIR, PAIR), PAIR)
        other = pl.ds(pl.multiple_of((2 * chip + 1 - place[1]) * PAIR, PAIR), PAIR)
        out[:, own] = held[:, own]
        out[:, other] = got[0, :, pair]


def mixed_kernel(n0, n1, n2, n3, nx, w_own, w_sib, m0, m1, m2, m3):
    half = nx.shape[1]
    weight = jnp.concatenate([w_own[...], w_sib[...]], axis=0)
    for m, (n, out) in enumerate(zip((n0, n1, n2, n3), (m0, m1, m2, m3))):
        rows = jnp.concatenate([n[:half, :], nx[m]], axis=1)
        out[...] = dims(rows, weight, 1, 0).astype(out.dtype)


def weight_kernel(*refs):
    packs, cots, outs = refs[:COLUMNS], refs[COLUMNS : 3 * COLUMNS], refs[3 * COLUMNS :]
    half = cots[0].shape[0]
    total = None
    for m in range(COLUMNS):
        for part in range(2):
            term = dims(packs[m][pl.ds(part * half, half), :], cots[2 * m + part][...], 0, 0)
            total = term if total is None else total + term
    outs[0][...] = total[: 2 * QUARTER]
    outs[1][...] = total[2 * QUARTER :].astype(bf16)


def gathered_kernel(scale, place, t0, t1, t2, t3, out):
    for m, t in enumerate((t0, t1, t2, t3)):
        column = lax.bitwise_xor(place[2], m)
        out[pl.ds(pl.multiple_of(column * QUARTER, QUARTER), QUARTER), :] = t[...].astype(f32) * scale


def finish_kernel(place, got, held, k_own, v_own, near, near_sib, far, far_sib, part_k, part_v, gq, gk, gv):
    fill_kernel(place, got, held, gq)
    outer_kernel(place, k_own, v_own, near, near_sib, far, far_sib, part_k, part_v, got, gk, gv)


def after(x, *earlier):
    return lax.optimization_barrier((x, *earlier))[0]


def on_device_planned(query_rows, key_rows, value_rows, norm_gain, out_weight, cotangent):
    query, key, value, cot = query_rows[0], key_rows[0], value_rows[0], cotangent[0]
    half, width = query.shape
    here, column = lax.axis_index("ctx"), lax.axis_index("dp")
    place = jnp.stack([here // 2, here % 2, column]).astype(jnp.int32)
    gain = norm_gain.reshape(1, width)
    heads = 2 * CHIPS
    state_shape = like((heads, HEAD, HEAD), bf16)
    state_flops = 2 * heads * 2 * half * HEAD * HEAD
    pack, full = like((2 * half, PAIR), bf16), like((half, width), bf16)
    part = like((half, width // 2), f32)
    step = 1024

    def column_spec(rows, columns):
        return pl.BlockSpec((rows, columns), lambda i: (0, i))

    def fixed(shape):
        return pl.BlockSpec(shape, lambda i: (0,) * len(shape))

    def sent(x, name, axis, pairs):
        with jax.named_scope("send_" + name):
            return lax.ppermute(x, axis, pairs)

    def to_sib(x, name):
        return sent(x, name, "ctx", [(i, i ^ 1) for i in range(2 * CHIPS)])

    def swapped(x, s, name):
        pairs = [(2 * c + e, 2 * (c ^ s) + e) for c in range(CHIPS) for e in range(2)]
        return sent(x, name, "ctx", pairs)

    def halfway(x, s, name):
        pairs = [(2 * c + e, 2 * (c + s) + e) for c in range(CHIPS) for e in range(2) if 0 <= c + s < CHIPS]
        return sent(x, name, "ctx", pairs)

    def across(x, m, name):
        return sent(x, name, "dp", [(d, d ^ m) for d in range(COLUMNS)])

    key_sib = to_sib(key, "key")
    value_sib = to_sib(value, "value")
    state = call(
        states_kernel, [state_shape], "states", (place, key, key_sib, value, value_sib), state_flops
    )[0]
    query_sib = to_sib(after(query, state), "query")
    near = swapped(state, 1, "near")
    pair_state = state + near
    far = halfway(pair_state, 2, "far")
    sib0 = to_sib(after(cot, state), "sib0")
    attended, *packs = after(call(
        attend_kernel,
        [like((2 * half, heads * HEAD), f32)] + [pack] * COLUMNS,
        "attend",
        (place, query, query_sib, key, key_sib, value, value_sib, near, far, gain),
        8 * state_flops,
        hint=0,
    ), sib0)
    quarter = lax.dynamic_slice(out_weight, (column * QUARTER, 0), (QUARTER, width))
    w2 = swapped(quarter, 2, "w2")
    w_first = jnp.concatenate([quarter, w2], axis=0)
    w_second = swapped(w_first, 1, "w_second")
    cot1 = across(cot, 1, "cot1")
    sib1 = to_sib(cot1, "sib1")
    cot2 = across(cot, 2, "cot2")
    sib2 = to_sib(after(cot2, far), "sib2")
    cot3 = across(after(cot, cot1, cot2), 3, "cot3")
    sib3 = to_sib(cot3, "sib3")
    cot_parts = [cot, sib0, cot1, sib1, cot2, sib2, cot3, sib3]
    d_packs = call(
        d_normed_kernel,
        [pack] * COLUMNS,
        "d_normed",
        (w_first, w_second, *cot_parts),
        2 * 8 * half * PAIR * width,
    )
    n1 = after(across(packs[1], 1, "n1"), *d_packs)
    n2 = after(across(packs[2], 2, "n2"), *d_packs)
    n3 = after(across(packs[3], 3, "n3"), *d_packs)
    n_got = (packs[0], n1, n2, n3)
    kept, given = call(
        weight_kernel,
        [like((2 * QUARTER, width), f32), like((2 * QUARTER, width), bf16)],
        "weight_terms",
        (*n_got, *cot_parts),
        2 * 8 * half * PAIR * width,
        grid=(width // step,),
        in_specs=[fixed((2 * half, PAIR))] * COLUMNS + [column_spec(half, step)] * (2 * COLUMNS),
        out_specs=[column_spec(2 * QUARTER, step)] * 2,
    )
    n_sib = to_sib(after(jnp.stack([n[half:] for n in n_got]), given), "n_sib")
    weight = jnp.concatenate([w_first, w_second], axis=0)
    w_sib = to_sib(after(weight, given), "w_sib")
    outs = call(
        mixed_kernel,
        [like((half, width), f32)] + [like((half, width), bf16)] * (COLUMNS - 1),
        "mixed_terms",
        (*n_got, n_sib, weight, w_sib),
        2 * 4 * half * 2 * PAIR * width,
        grid=(width // step,),
        in_specs=[fixed((2 * half, PAIR))] * COLUMNS
        + [fixed((COLUMNS, half, PAIR))]
        + [column_spec(PAIR, step)] * 2,
        out_specs=[column_spec(half, step)] * COLUMNS,
    )
    mixed1 = across(outs[1], 1, "mixed1")
    mixed2 = across(outs[2], 2, "mixed2")
    mixed3 = across(outs[3], 3, "mixed3")
    mixed_got = [mixed1, mixed2, mixed3]
    mixed = outs[0]
    for x in mixed_got:
        mixed = mixed + x.astype(f32)
    mixed = mixed.astype(bf16)
    d1 = across(d_packs[1], 1, "d1")
    d2 = across(d_packs[2], 2, "d2")
    d3 = across(d_packs[3], 3, "d3")
    d_got = (d_packs[0], d1, d2, d3)
    d_attended, d_state = call(
        d_attend_kernel,
        [like((2 * half, heads * HEAD), bf16), state_shape],
        "d_attend",
        (place, query, query_sib, attended, gain, *d_got),
        2 * state_flops,
    )
    gq, part_k, part_v, parts_sent = call(
        inner_kernel,
        [full, part, part, like((3, half, width // 2), bf16)],
        "inner",
        (place, query, query_sib, key, key_sib, value, value_sib, near, far, after(d_attended, mixed)),
        14 * state_flops,
    )
    parts_got = to_sib(parts_sent, "parts")
    terms = swapped(given, 1, "terms")
    d_near = swapped(after(d_state, terms), 1, "d_near")
    d_near_sib = to_sib(d_near, "d_near_sib")
    d_pair_state = d_state + d_near
    d_far = halfway(d_pair_state, -2, "d_far")
    d_far_sib = to_sib(d_far, "d_far_sib")
    pair = kept + terms.astype(f32)
    pair_terms = after(swapped(pair[QUARTER:].astype(bf16), 2, "pair_terms"), gq)
    share = (pair[:QUARTER] + pair_terms.astype(f32)).astype(bf16)
    share1 = across(share, 1, "share1")
    share2 = across(share, 2, "share2")
    share3 = across(share, 3, "share3")
    scale = 1.0 / math.sqrt(lax.axis_size("dp") * lax.axis_size("ctx") * half)
    grad_queries, *grad_kv = call(
        finish_kernel,
        [full, full, full],
        "finish",
        (place, parts_got, gq, key, value, d_near, d_near_sib, d_far, d_far_sib, part_k, part_v),
        2 * state_flops,
    )
    grad_weight = call(
        functools.partial(gathered_kernel, scale),
        [like(out_weight.shape, f32)],
        "grad_weight",
        (place, *(share, share1, share2, share3)),
        0,
    )[0]
    return (mixed[None], grad_queries[None], grad_kv[0][None], grad_kv[1][None], grad_weight)


def on_device(query_rows, key_rows, value_rows, norm_gain, out_weight, cotangent):
    fits = (
        lax.axis_size("dp") == COLUMNS
        and lax.axis_size("ctx") == 2 * CHIPS
        and out_weight.shape[0] == PAIR
        and out_weight.shape[1] == 2 * CHIPS * PAIR
        and query_rows.shape[1] == HEAD
    )
    path = on_device_planned if fits else on_device_general
    return path(query_rows, key_rows, value_rows, norm_gain, out_weight, cotangent)


def solution(mesh):
    return jax.shard_map(
        on_device,
        mesh=mesh,
        in_specs=(
            P("dp", "ctx", None),
            P("dp", "ctx", None),
            P("dp", "ctx", None),
            P(),
            P("ctx", None),
            P("dp", "ctx", None),
        ),
        out_specs=(
            P("dp", "ctx", None),
            P("dp", "ctx", None),
            P("dp", "ctx", None),
            P("dp", "ctx", None),
            P("ctx", None),
        ),
        check_vma=False,
    )
```
